32 devices in a mesh: prow: 4 (over z), pcol: 8 (over y, x, core).
Axes of the slice: x: 2, y: 2, z: 4, core: 2. Of those that a mesh axis runs over, the one named last changes fastest.
Arguments:
- ancestor_inv: float32 [16384, 16384], P('prow', 'pcol'), may hold values from -0.15625 to 0.15625
- l_scaled: float32 [2, 1536, 512], P(None, 'prow'), may hold values from -0.9 to 0.9
- diag_inv: float32 [2, 512, 512], replicated, may hold values from -6 to 6
- tile_lists: int32 [2, 6], replicated, may hold values from 0 to 63, as said below
Outputs:
- offdiag: float32 [2, 1536, 512], P(None, ('prow', 'pcol'))
- diag_block: float32 [2, 512, 512], replicated
The draws below stay inside these ranges and needn't reach their ends.
Inputs may be any that keep to these rules, and one draw needn't show every extreme that they name: `tile_lists`: each row holds 6 different tile numbers; tile 0 and tile 64 - 1 are in every row.
All inputs are finite; a program needn't handle non-finite values.
Results may differ from the reference program's by a relative error of at most 0.0001.
Values sent between devices are 32-bit elements; how exact they have to be, the bound alone decides.
A program may use at most 192 MiB of HBM per device.

```python
import jax
import jax.numpy as jnp
from jax import lax

TILE = 256
W = 512
NT = 64
NS = 6
NSUP = 2
ORDER = 16384
ROWS = 1536


def draw_tile_lists(key, part):

    def single(sub):
        first, second = jax.random.split(sub)
        middle = 1 + jax.random.permutation(first, NT - 2)[:NS - 2]
        ends = jnp.array([0, NT - 1], dtype=jnp.int32)
        whole = jnp.concatenate([ends, middle.astype(jnp.int32)])
        return jax.random.permutation(second, whole)
    keys = jax.random.split(jax.random.fold_in(key, 7), NSUP)
    return jax.vmap(single)(keys).astype(jnp.int32)


def block_levels(stream_key, shape, pieces, least, top_value):
    loudness = 1.0
    for axis_at, parts in pieces:
        draws = jax.random.uniform(jax.random.fold_in(jax.random.fold_in(stream_key, 6), axis_at), (parts,), jnp.float32, least / len(pieces), top_value / len(pieces))
        loudness = loudness * jnp.repeat(jnp.exp(draws), shape[axis_at] // parts).reshape((-1,) + (1,) * (len(shape) - 1 - axis_at))
    return loudness


def scatter_about(rng, dims, width, most, cuts=(), kind=jnp.bfloat16):
    drawn = jax.random.normal(rng, dims, jnp.float32) * width
    if len(cuts) > 0:
        drawn = block_levels(rng, dims, cuts, -0.22, 0.18) * drawn
    return jnp.clip(drawn, min=-most, max=most).astype(kind)


def setup_inputs(seed: int = 0) -> dict:
    key_list = jax.random.split(jax.random.key(seed), 5)
    return {
        "ancestor_inv": scatter_about(key_list[0], (ORDER, ORDER), (NS * TILE) ** -0.5, 0.15625, ((0, 4), (1, 8)), jnp.float32),
        "l_scaled": scatter_about(key_list[1], (NSUP, ROWS, W), 0.15, 0.9, ((1, 4),), jnp.float32),
        "diag_inv": scatter_about(key_list[2], (NSUP, W, W), 1.0, 6.0, (), jnp.float32),
        "tile_lists": draw_tile_lists(jax.random.fold_in(key_list[4], 71), 0),
    }


def reference(ancestor_inv, l_scaled, diag_inv, tile_lists):
    offs = []
    diags = []
    within = jnp.arange(TILE, dtype=jnp.int32)
    for index in range(NSUP):
        rows_k = (tile_lists[index][:, None] * TILE + within[None, :]).reshape(-1).astype(jnp.int32)
        block = ancestor_inv[rows_k][:, rows_k]
        result = -jnp.dot(block, l_scaled[index], precision=lax.Precision.HIGHEST, preferred_element_type=jnp.float32)
        offs.append(result)
        term = jnp.dot(l_scaled[index].T, result, precision=lax.Precision.HIGHEST, preferred_element_type=jnp.float32)
        diags.append(diag_inv[index] - term)
    return jnp.stack(offs), jnp.stack(diags)
```

```python
import functools

import jax
import jax.numpy as jnp
from jax import lax
from jax.experimental import pallas as pl
from jax.experimental.pallas import tpu as pltpu
from jax.sharding import PartitionSpec as P

TILE = 256
W = 512
NS = 6
NSUP = 2
MESH = pl.DeviceIdType.MESH


def place(stage):
    row = lax.axis_index("prow")
    col = lax.axis_index("pcol")
    core = lax.rem(col, 2)
    chip = col // 2
    if stage == "row":
        return row, lambda m: (m, col)
    if stage == "chip":
        return chip, lambda m: (row, m * 2 + core)
    return core, lambda m: (row, chip * 2 + m)


def enter(peers):
    barrier = pltpu.get_barrier_semaphore()
    for peer in peers:
        pl.semaphore_signal(barrier, inc=1, device_id=peer, device_id_type=MESH)
    pl.semaphore_wait(barrier, len(peers))


def others(stage, size):
    me, device = place(stage)
    return [device(lax.rem(me + step, size)) for step in range(1, size)]


def send(src, dst, send_sem, recv_sem, peer):
    copy = pltpu.make_async_remote_copy(
        src_ref=src,
        dst_ref=dst,
        send_sem=send_sem,
        recv_sem=recv_sem,
        device_id=peer,
        device_id_type=MESH,
    )
    copy.start()
    return copy


def scatter_kernel(
    nrow, nchip, x_ref, y_ref, x_out, y_out, core_x, core_y, held, chip_in, sums, row_in, *sems
):
    core_send, core_recv, chip_send, chip_recv, row_send, row_recv = sems
    row, _ = place("row")
    chip, _ = place("chip")
    core, _ = place("core")
    rows, chips, cores = others("row", nrow), others("chip", nchip), others("core", 2)
    enter(rows + chips + cores)
    count = x_ref.shape[-2]
    pieces = [(step, sup) for step in [*range(1, nrow), 0] for sup in range(NSUP)]
    owners = [lax.rem(row + step, nrow) for step, _ in pieces]
    from_core = []
    for at, (_, sup) in enumerate(pieces):
        to = owners[at]
        from_core.append(
            [
                send(
                    src.at[sup, to, :, 1 - core],
                    dst.at[at],
                    core_send.at[at, which],
                    core_recv.at[at, which],
                    cores[0],
                )
                for which, (src, dst) in enumerate(((x_ref, core_x), (y_ref, core_y)))
            ]
        )
    from_chips = []
    from_rows = []

    def finish(at):
        step, sup = pieces[at]
        for copy in from_chips[at]:
            copy.wait_recv()
        total = held[at, chip]
        for near in range(nchip - 1):
            total += chip_in[at, near]
        sums[at] = total
        if step > 0:
            from_rows.append(
                send(
                    sums.at[at],
                    row_in.at[at],
                    row_send.at[at],
                    row_recv.at[at],
                    rows[step - 1],
                )
            )

    for at, (_, sup) in enumerate(pieces):
        for copy in from_core[at]:
            copy.wait_recv()
        held[at, :, :count] = x_ref[sup, owners[at], :, core] + core_x[at]
        held[at, :, count:] = y_ref[sup, owners[at], :, core] + core_y[at]
        from_chips.append(
            [
                send(
                    held.at[at, lax.rem(chip + near + 1, nchip)],
                    chip_in.at[at, near],
                    chip_send.at[at, near],
                    chip_recv.at[at, near],
                    peer,
                )
                for near, peer in enumerate(chips)
            ]
        )
        if at >= 2:
            finish(at - 2)
    finish(len(pieces) - 2)
    finish(len(pieces) - 1)
    for copy in from_rows:
        copy.wait_recv()
    for sup in range(NSUP):
        total = sums[(nrow - 1) * NSUP + sup]
        for step in range(nrow - 1):
            total += row_in[step * NSUP + sup]
        x_out[sup] = total[:count]
        y_out[sup] = total[count:]
    for group in from_core + from_chips + [from_rows]:
        for copy in group:
            copy.wait_send()


def scatter(x, y, nrow, nchip, collective_id):
    count, part = x.shape[-2], y.shape[-2]
    n = nrow * NSUP
    f32 = jnp.float32
    vmem = pl.BlockSpec(memory_space=pltpu.VMEM)
    core, chip, row = (n, 2), (n, nchip - 1), (n - NSUP,)
    return pl.pallas_call(
        functools.partial(scatter_kernel, nrow, nchip),
        out_shape=[
            jax.ShapeDtypeStruct((NSUP, count, W), f32),
            jax.ShapeDtypeStruct((NSUP, part, W), f32),
        ],
        in_specs=[vmem, vmem],
        out_specs=[vmem, vmem],
        scratch_shapes=[
            pltpu.VMEM((n, nchip, count, W), f32),
            pltpu.VMEM((n, nchip, part, W), f32),
            pltpu.VMEM((n, nchip, count + part, W), f32),
            pltpu.VMEM((n, nchip - 1, count + part, W), f32),
            pltpu.VMEM((n, count + part, W), f32),
            pltpu.VMEM((n - NSUP, count + part, W), f32),
            *(pltpu.SemaphoreType.DMA(s) for s in (core, core, chip, chip, row, row)),
        ],
        compiler_params=pltpu.CompilerParams(
            collective_id=collective_id,
            has_side_effects=True,
            vmem_limit_bytes=44 * 1024 * 1024,
        ),
    )(x, y)


def gather_kernel(nrow, nchip, known, x_ref, out_ref, *sems):
    row_send, row_recv, chip_send, chip_recv, core_send, core_recv = sems
    row, _ = place("row")
    chip, _ = place("chip")
    core, _ = place("core")
    rows, chips, cores = others("row", nrow), others("chip", nchip), others("core", 2)
    enter(rows + chips + cores)
    started = []

    def forward(*args):
        started.append(send(*args))
        return started[-1]

    mine = out_ref.at[:, row, chip, core]
    from_rows = [
        forward(x_ref, mine, row_send.at[step], row_recv.at[step], peer)
        for step, peer in enumerate(rows)
    ]
    from_chips = []
    last = []
    for near in range(1 if known else 0, nrow):
        src = x_ref
        slot = mine
        if near > 0:
            from_rows[near - 1].wait_recv()
            slot = out_ref.at[:, lax.rem(row - near + nrow, nrow), chip, core]
            src = slot
        for step, peer in enumerate(chips):
            from_chips.append(
                (
                    near,
                    step + 1,
                    forward(src, slot, chip_send.at[step, near], chip_recv.at[step, near], peer),
                )
            )
        last.append(forward(src, slot, core_send.at[0, near], core_recv.at[0, near], cores[0]))
    for near, step, copy in from_chips:
        copy.wait_recv()
        slot = out_ref.at[
            :, lax.rem(row - near + nrow, nrow), lax.rem(chip - step + nchip, nchip), core
        ]
        last.append(
            forward(slot, slot, core_send.at[step, near], core_recv.at[step, near], cores[0])
        )
    for copy in last:
        copy.wait_recv()
    for copy in started:
        copy.wait_send()


def gather(x, nrow, nchip, collective_id, plane=None):
    shape = (x.shape[0], nrow, nchip, 2) + x.shape[1:]
    row, chip, core = ((nrow - 1,), (nchip - 1, nrow), (nchip, nrow))
    full = pl.pallas_call(
        functools.partial(gather_kernel, nrow, nchip, plane is not None),
        out_shape=jax.ShapeDtypeStruct(shape, x.dtype),
        in_specs=[pl.BlockSpec(memory_space=pl.ANY)],
        out_specs=pl.BlockSpec(memory_space=pl.ANY),
        scratch_shapes=[
            pltpu.SemaphoreType.DMA(n) for n in (row, row, chip, chip, core, core)
        ],
        compiler_params=pltpu.CompilerParams(
            collective_id=collective_id, has_side_effects=True
        ),
    )(x)
    if plane is not None:
        plane = plane.reshape(x.shape[0], 1, nchip, 2, *x.shape[1:])
        return lax.dynamic_update_slice(full, plane, (0, place("row")[0], 0, 0, 0, 0))
    where = (0, place("row")[0], place("chip")[0], place("core")[0], 0, 0)
    return lax.dynamic_update_slice(full, x[:, None, None, None], where)


def dot(a, b, contract):
    def split(x):
        high = x.astype(jnp.bfloat16)
        return high, (x - high.astype(jnp.float32)).astype(jnp.bfloat16)

    def one(x, y):
        return lax.dot_general(
            x, y, ((contract, (0,)), ((), ())), preferred_element_type=jnp.float32
        )

    a_high, a_low = split(a)
    b_high, b_low = split(b)
    return one(a_low, b_high) + one(a_high, b_low) + one(a_high, b_high)


def product_kernel(rows_ref, cols_ref, *refs):
    *tiles, l_ref, p_ref, d_ref = refs
    sup, i = pl.program_id(0), pl.program_id(1)
    row_hit = rows_ref[sup, i] >= 0

    @pl.when(i == 0)
    def _():
        d_ref[...] = jnp.zeros_like(d_ref)

    p_ref[...] = jnp.zeros_like(p_ref)

    @pl.when(row_hit)
    def _():
        for j, a_ref in enumerate(tiles):

            @pl.when(cols_ref[sup, j] >= 0)
            def _():
                p_ref[0] -= dot(a_ref[...], l_ref[0, j * TILE:(j + 1) * TILE, :], (1,))

        block = l_ref[0, pl.ds(pl.multiple_of(i * TILE, TILE), TILE), :]
        d_ref[0] += dot(block, p_ref[0], (0,))


def products(rows, cols, ancestor, lfull):
    def tile(j):
        def index(sup, i, rows_ref, cols_ref):
            row, col = rows_ref[sup, i], cols_ref[sup, j]
            hit = (row >= 0) & (col >= 0)
            return jnp.where(hit, row, 0), jnp.where(hit, col, 0)

        return pl.BlockSpec((TILE, TILE), index)

    total = lfull.shape[1]
    return pl.pallas_call(
        product_kernel,
        out_shape=(
            jax.ShapeDtypeStruct((NSUP, total, W), jnp.float32),
            jax.ShapeDtypeStruct((NSUP, W, W), jnp.float32),
        ),
        grid_spec=pltpu.PrefetchScalarGridSpec(
            num_scalar_prefetch=2,
            grid=(NSUP, NS),
            in_specs=[tile(j) for j in range(NS)]
            + [pl.BlockSpec((1, total, W), lambda sup, i, *_: (sup, 0, 0))],
            out_specs=[
                pl.BlockSpec((1, TILE, W), lambda sup, i, *_: (sup, i, 0)),
                pl.BlockSpec((1, W, W), lambda sup, i, *_: (sup, 0, 0)),
            ],
        ),
        compiler_params=pltpu.CompilerParams(vmem_limit_bytes=40 * 1024 * 1024),
    )(rows, cols, *[ancestor] * NS, lfull)


ROW_TILES = 16
COL_TILES = 8
UNIT = 16


def flip(value, bit):
    return value + bit - 2 * bit * lax.rem(lax.div(value, bit), 2)


def split(x):
    high = x.astype(jnp.bfloat16)
    return high, (x - high.astype(jnp.float32)).astype(jnp.bfloat16)


def dot3(a, b, contract):
    def one(x, y):
        return lax.dot_general(
            x, y, ((contract, (0,)), ((), ())), preferred_element_type=jnp.float32
        )

    (a_high, a_low), (b_high, b_low) = a, b
    return one(a_low, b_high) + one(a_high, b_low) + one(a_high, b_high)


def fused_kernel(rcap, ccap, *refs):
    t_ref, a_ref, l_ref, d_ref, off_ref, diag_ref, a_buf, b_high, b_low, tab, dinv = refs[:11]
    local_sem, send_sem, recv_sem = refs[-3:]
    per_sup = refs[11:-3]
    groups = [per_sup[i * NSUP:(i + 1) * NSUP] for i in range(len(per_sup) // NSUP)]
    l_buf, p_buf, core_in, held, chip_in, total, d_buf, d_core, d_sum, d_in, e_buf, e_in, f_buf = groups
    row = lax.axis_index("prow")
    col = lax.axis_index("pcol")
    core = lax.rem(col, 2)
    chip = lax.div(col, 2)
    rows = [row, flip(row, 1), flip(row, 2), flip(flip(row, 1), 2)]
    chips = [chip, flip(chip, 1), flip(chip, 2), flip(flip(chip, 1), 2)]
    sibling = (row, chip * 2 + 1 - core)

    def on_row(s):
        return rows[s], col

    def on_chip(d):
        return row, chips[d] * 2 + core

    def across(d):
        return row, chips[d] * 2 + 1 - core

    started = []

    def send(src, dst, peer):
        at = len(started)
        copy = pltpu.make_async_remote_copy(
            src_ref=src,
            dst_ref=dst,
            send_sem=send_sem.at[at],
            recv_sem=recv_sem.at[at],
            device_id=peer,
            device_id_type=MESH,
        )
        copy.start()
        started.append(copy)
        return copy

    local = []

    def fetch(src, dst):
        copy = pltpu.make_async_copy(src, dst, local_sem.at[len(local)])
        copy.start()
        local.append(copy)
        return copy

    quarter = l_ref.shape[1]
    half = quarter // 2
    own_l = [
        [
            fetch(l_ref.at[sup, :, :, :, w * 128:(w + 1) * 128],
                  l_buf[sup].at[w, pl.ds(row * quarter, quarter)])
            for w in range(4)
        ]
        for sup in range(NSUP)
    ]
    own_a = [
        fetch(a_ref.at[:, :, j * TILE:(j + 1) * TILE], a_buf.at[j]) for j in range(COL_TILES)
    ]
    d_rows = 256 * core + 64 * row
    lanes = pl.ds(pl.multiple_of(chip * 128, 128), 128)
    own_d = fetch(d_ref.at[:, pl.ds(pl.multiple_of(d_rows, 64), 64), lanes], dinv)

    peers = [on_row(s) for s in (1, 2, 3)] + [on_chip(d) for d in (1, 2, 3)]
    peers += [sibling] + [across(d) for d in (1, 2, 3)]
    enter(peers)

    def piece(sup, s, d, begin=0, size=None):
        size = half if size is None else size
        return l_buf[sup].at[chips[d], pl.ds(rows[s] * quarter + core * half + begin, size)]

    from_rows = [
        [
            send(l_ref.at[sup, pl.ds(core * half, half), :, :, lanes],
                 piece(sup, 0, 0), on_row(s))
            for s in (1, 2, 3)
        ]
        for sup in range(NSUP)
    ]
    from_x, from_y, from_far, from_sib = ([[] for _ in range(NSUP)] for _ in range(4))

    def spread_rows(sup):
        for s in (1, 2, 3):
            from_rows[sup][s - 1].wait_recv()
            block = piece(sup, s, 0)
            from_x[sup].append(send(block, block, on_chip(1)))
            from_y[sup].append(send(block, block, on_chip(2)))
            from_sib[sup].append(send(block, block, sibling))

    def spread_chips(sup):
        part = half // 2
        for s in (1, 2, 3):
            from_x[sup][s - 1].wait_recv()
            block = piece(sup, s, 1, 0, part)
            from_far[sup].append((s, 0, send(block, block, on_chip(2))))
            from_y[sup][s - 1].wait_recv()
            block = piece(sup, s, 2, part, part)
            from_far[sup].append((s, part, send(block, block, on_chip(1))))
            for d in (1, 2):
                block = piece(sup, s, d)
                from_sib[sup].append(send(block, block, sibling))

    def finish_l(sup):
        part = half // 2
        for s, begin, copy in from_far[sup]:
            copy.wait_recv()
            block = piece(sup, s, 3, begin, part)
            from_sib[sup].append(send(block, block, sibling))
        for copy in from_sib[sup]:
            copy.wait_recv()
        for copy in own_l[sup]:
            copy.wait()

    width = 2 * rcap + 2 * NS + 3 * ccap

    def make_table(sup):
        tiles = [t_ref[sup, k] for k in range(NS)]

        def ranked(base, extent, cap):
            seen = jnp.int32(0)
            found = []
            for k in range(NS):
                at = tiles[k] - base
                hit = ((at >= 0) & (at < extent)).astype(jnp.int32)
                found.append((at, hit, seen))
                seen = seen + hit
            slots = []
            for s in range(cap):
                tile, pos, valid = jnp.int32(0), jnp.int32(0), jnp.int32(0)
                for k, (at, hit, rank) in enumerate(found):
                    here = hit * (rank == s).astype(jnp.int32)
                    tile = tile + here * at
                    pos = pos + here * k
                    valid = valid + here
                slots.append((tile, pos, valid))
            return slots, found

        slots, found = ranked(row * ROW_TILES, ROW_TILES, rcap)
        base = sup * width
        for s, (tile, pos, valid) in enumerate(slots):
            tab[base + s] = tile + (valid - 1) * ROW_TILES
            tab[base + rcap + s] = pos
        base += 2 * rcap
        for k, (_, hit, rank) in enumerate(found):
            tab[base + k] = hit
            tab[base + NS + k] = jnp.minimum(rank, rcap - 1)
        base += 2 * NS
        slots, _ = ranked(col * COL_TILES, COL_TILES, ccap)
        for s, (tile, pos, valid) in enumerate(slots):
            tab[base + s] = tile
            tab[base + ccap + s] = pos
            tab[base + 2 * ccap + s] = valid

    from_core = [[] for _ in range(NSUP)]

    def product(sup):
        base = sup * width
        cols = base + 2 * rcap + 2 * NS
        for t in range(ccap):
            pos = tab[cols + ccap + t]
            for w in range(4):
                block = l_buf[sup][w, pl.ds(pos * UNIT, UNIT)].reshape(TILE, 128)
                high, low = split(block)
                b_high[t * TILE:(t + 1) * TILE, w * 128:(w + 1) * 128] = high
                b_low[t * TILE:(t + 1) * TILE, w * 128:(w + 1) * 128] = low

        @pl.loop(0, rcap)
        def _(s):
            at = tab[base + s]
            tiles = []
            for t in range(ccap):
                hit = (at >= 0) & (tab[cols + 2 * ccap + t] > 0)
                block = a_buf[tab[cols + t], jnp.maximum(at, 0)]
                tiles.append(jnp.where(hit, block, 0.0))
            a = split(jnp.concatenate(tiles, axis=1))
            result = dot3(a, (b_high[...], b_low[...]), (1,))
            for w in range(4):
                block = result[:, w * 128:(w + 1) * 128].reshape(UNIT, 2, 8, 128)
                p_buf[sup][0, w, s] = block[:, 0]
                p_buf[sup][1, w, s] = block[:, 1]

        for d in (1, 2, 3, 0):
            from_core[sup].append(
                send(p_buf[sup].at[1 - core, chips[d]], core_in[sup].at[chips[d]], sibling)
            )

    from_chips = [[] for _ in range(NSUP)]

    def reduce_send(sup):
        for at, d in enumerate((1, 2, 3, 0)):
            from_core[sup][at].wait_recv()
            w = chips[d]
            held[sup][w] = p_buf[sup][core, w] + core_in[sup][w]
            if d > 0:
                from_chips[sup].append(
                    send(held[sup].at[w], chip_in[sup].at[d - 1], on_chip(d))
                )

    from_d = [None] * NSUP

    def reduce_finish(sup):
        for copy in from_chips[sup]:
            copy.wait_recv()
        total[sup][...] = held[sup][chip] + chip_in[sup][0] + chip_in[sup][1] + chip_in[sup][2]
        base = sup * width
        picked = []
        for s in range(rcap):
            pos = tab[base + rcap + s]
            picked.append(
                jnp.concatenate(
                    [
                        l_buf[sup][w, pl.ds(pos * UNIT, UNIT), core].reshape(128, 128)
                        for w in range(4)
                    ],
                    axis=1,
                )
            )
        left = split(jnp.concatenate(picked, axis=0))
        right = split(total[sup][...].reshape(rcap * 128, 128))
        d_buf[sup][...] = dot3(left, right, (0,)).reshape(2, 256, 128)
        from_d[sup] = send(d_buf[sup].at[1 - core], d_core[sup], sibling)

    from_e = [[] for _ in range(NSUP)]

    def listed(sup, to, put):
        base = sup * width + 2 * rcap
        for j in range(3):
            unit = 3 * to + j
            k = lax.div(unit, 2)
            begin = pl.multiple_of(8 * lax.rem(unit, 2), 8)
            block = total[sup][tab[base + NS + k], pl.ds(begin, 8)]
            put(j, jnp.where(tab[base + k] > 0, block, 0.0))

    def exchange(sup):
        for s in (1, 2, 3):
            def put(j, block):
                e_buf[sup][s - 1, 8 * j:8 * j + 8] = block

            listed(sup, rows[s], put)
            from_e[sup].append(
                send(e_buf[sup].at[s - 1], e_in[sup].at[s - 1], on_row(s))
            )

    from_dr = [[] for _ in range(NSUP)]

    def diag_rows(sup):
        from_d[sup].wait_recv()
        d_sum[sup][...] = (d_buf[sup][core] + d_core[sup][...]).reshape(4, 64, 128)
        for s in (1, 2, 3):
            from_dr[sup].append(
                send(d_sum[sup].at[rows[s]], d_in[sup].at[s - 1], on_row(s))
            )

    from_g = [[] for _ in range(NSUP)]

    def diag_piece(sup):
        for copy in from_dr[sup]:
            copy.wait_recv()
        mine = diag_ref.at[sup, pl.ds(pl.multiple_of(d_rows, 64), 64), lanes]
        value = d_sum[sup][row] + d_in[sup][0] + d_in[sup][1] + d_in[sup][2]
        mine[...] = dinv[sup] + value
        for s in (1, 2, 3):
            from_g[sup].append(send(mine, mine, on_row(s)))

    from_gc = [[] for _ in range(NSUP)]
    from_gs = [[] for _ in range(NSUP)]

    def diag_block(sup, d):
        at = pl.ds(pl.multiple_of(chips[d] * 128, 128), 128)
        return diag_ref.at[sup, pl.ds(pl.multiple_of(256 * core, 256), 256), at]

    def diag_chips(sup):
        for copy in from_g[sup]:
            copy.wait_recv()
        block = diag_block(sup, 0)
        for d in (1, 2, 3):
            from_gc[sup].append(send(block, block, on_chip(d)))
        from_gs[sup].append(send(block, block, sibling))

    def diag_cores(sup):
        for d in (1, 2, 3):
            from_gc[sup][d - 1].wait_recv()
            block = diag_block(sup, d)
            from_gs[sup].append(send(block, block, sibling))

    from_o = [[] for _ in range(NSUP)]

    def owners(sup):
        for copy in from_e[sup]:
            copy.wait_recv()

        def put(j, block):
            at = slice(8 * j, 8 * j + 8)
            rest = e_in[sup][0, at] + e_in[sup][1, at] + e_in[sup][2, at]
            f_buf[sup][at] = -(block + rest)

        listed(sup, row, put)
        place_at = off_ref.at[sup, :, core, :, lanes]

        def share(to):
            return f_buf[sup].at[pl.ds(3 * to, 3)]

        for d in (1, 2, 3):
            for peer in (on_chip(d), across(d)):
                from_o[sup].append(send(share(peer[1]), place_at, peer))
        from_o[sup].append(send(share(sibling[1]), place_at, sibling))
        off_ref[sup, :, core, :, lanes] = f_buf[sup][pl.ds(3 * col, 3)]

    for sup in range(NSUP):
        make_table(sup)
    spread_rows(0)
    spread_chips(0)
    spread_rows(1)
    finish_l(0)
    for copy in own_a:
        copy.wait()
    product(0)
    spread_chips(1)
    reduce_send(0)
    finish_l(1)
    product(1)
    reduce_finish(0)
    exchange(0)
    reduce_send(1)
    diag_rows(0)
    reduce_finish(1)
    own_d.wait()
    diag_piece(0)
    diag_rows(1)
    exchange(1)
    diag_chips(0)
    owners(0)
    diag_piece(1)
    diag_cores(0)
    diag_chips(1)
    owners(1)
    diag_cores(1)
    for group in from_gs + from_o:
        for copy in group:
            copy.wait_recv()
    for copy in started:
        copy.wait_send()


def fused(rcap, ccap, tile_lists, ancestor, l_scaled, diag_inv):
    f32 = jnp.float32
    total_rows = l_scaled.shape[1] * 4
    units = total_rows // UNIT
    view = l_scaled.reshape(NSUP, l_scaled.shape[1] // UNIT, 2, 8, W)
    any_space = pl.BlockSpec(memory_space=pl.ANY)
    vmem = pl.BlockSpec(memory_space=pltpu.VMEM)
    block = (rcap, UNIT, 8, 128)
    per_sup = [
        (4, units, 2, 8, 128),
        (2, 4) + block,
        (4,) + block,
        (4,) + block,
        (3,) + block,
        block,
        (2, 256, 128),
        (256, 128),
        (4, 64, 128),
        (3, 64, 128),
        (3, 24, 8, 128),
        (3, 24, 8, 128),
        (24, 8, 128),
    ]
    scratch = [
        pltpu.VMEM((COL_TILES, ROW_TILES, TILE, TILE), f32),
        pltpu.VMEM((ccap * TILE, W), jnp.bfloat16),
        pltpu.VMEM((ccap * TILE, W), jnp.bfloat16),
        pltpu.SMEM((NSUP * (2 * rcap + 2 * NS + 3 * ccap),), jnp.int32),
        pltpu.VMEM((NSUP, 64, 128), f32),
    ]
    for shape in per_sup:
        scratch += [pltpu.VMEM(shape, f32)] * NSUP
    sends = NSUP * (3 + 6 + 6 + 15 + 4 + 3 + 1 + 3 + 3 + 3 + 3 + 4 + 7)
    scratch += [
        pltpu.SemaphoreType.DMA((4 * NSUP + COL_TILES + 1,)),
        pltpu.SemaphoreType.DMA((sends,)),
        pltpu.SemaphoreType.DMA((sends,)),
    ]
    off, diag = pl.pallas_call(
        functools.partial(fused_kernel, rcap, ccap),
        out_shape=[
            jax.ShapeDtypeStruct((NSUP, 3, 2, 8, W), f32),
            jax.ShapeDtypeStruct((NSUP, W, W), f32),
        ],
        in_specs=[pl.BlockSpec(memory_space=pltpu.SMEM), any_space, any_space, any_space],
        out_specs=[vmem, vmem],
        scratch_shapes=scratch,
        compiler_params=pltpu.CompilerParams(
            collective_id=6 + rcap,
            has_side_effects=True,
            vmem_limit_bytes=60 * 1024 * 1024,
        ),
    )(tile_lists, ancestor.reshape(ROW_TILES, TILE, -1), view, diag_inv)
    return off.reshape(NSUP, 48, W), diag


def most(tile_lists, extent):
    ranges = jnp.arange(ROW_TILES * 4 // extent, dtype=jnp.int32)
    held = (tile_lists[:, :, None] // extent == ranges).astype(jnp.int32)
    return jnp.max(jnp.sum(held, axis=1))


def per_device(nrow, ncol, ancestor_inv, l_scaled, diag_inv, tile_lists):
    if (nrow, ncol) == (4, 8):
        args = (tile_lists, ancestor_inv, l_scaled, diag_inv)
        few = most(tile_lists, ROW_TILES) <= 4
        few &= most(tile_lists, COL_TILES) <= 3
        return lax.cond(
            few,
            functools.partial(fused, 4, 3),
            functools.partial(fused, NS - 1, NS - 1),
            *args,
        )
    return stepwise(nrow, ncol, ancestor_inv, l_scaled, diag_inv, tile_lists)


def stepwise(nrow, ncol, ancestor_inv, l_scaled, diag_inv, tile_lists):
    nchip = ncol // 2
    tile_rows = ancestor_inv.shape[0] // TILE
    tile_cols = ancestor_inv.shape[1] // TILE
    row_pos = lax.axis_index("prow")
    col_pos = lax.axis_index("pcol")
    count = l_scaled.shape[1] // ncol
    part = W // (nrow * ncol)
    total = l_scaled.shape[1] * nrow

    share = lax.dynamic_slice_in_dim(l_scaled, col_pos * count, count, 1)
    lfull = gather(share, nrow, nchip, 1, l_scaled).reshape(NSUP, total, W)

    rows = tile_lists - row_pos * tile_rows
    rows = jnp.where((rows >= 0) & (rows < tile_rows), rows, -1)
    cols = tile_lists - col_pos * tile_cols
    cols = jnp.where((cols >= 0) & (cols < tile_cols), cols, -1)
    rows = jnp.where(jnp.max(cols, axis=1, keepdims=True) >= 0, rows, -1)
    partial, terms = products(rows, cols, ancestor_inv, lfull)

    mine, term = scatter(
        partial.reshape(NSUP, nrow, nchip, 2, count, W),
        terms.reshape(NSUP, nrow, nchip, 2, part, W),
        nrow,
        nchip,
        2,
    )
    diag = gather(term, nrow, nchip, 5).reshape(NSUP, W, W)
    return mine, diag_inv - diag


def solution(mesh):
    placed = (P("prow", "pcol"), P(None, "prow", None), P(), P())
    return jax.shard_map(
        functools.partial(per_device, mesh.shape["prow"], mesh.shape["pcol"]),
        mesh=mesh,
        in_specs=placed,
        out_specs=(P(None, ("prow", "pcol"), None), P()),
        check_vma=False,
    )
```

```python
import functools

import jax
import jax.numpy as jnp
from jax import lax
from jax.experimental import pallas as pl
from jax.experimental.pallas import tpu as pltpu
from jax.sharding import PartitionSpec as P

TILE = 256
W = 512
NS = 6
NSUP = 2
MESH = pl.DeviceIdType.MESH


def place(stage):
    row = lax.axis_index("prow")
    col = lax.axis_index("pcol")
    core = lax.rem(col, 2)
    chip = col // 2
    if stage == "row":
        return row, lambda m: (m, col)
    if stage == "chip":
        return chip, lambda m: (row, m * 2 + core)
    return core, lambda m: (row, chip * 2 + m)


def enter(peers):
    barrier = pltpu.get_barrier_semaphore()
    for peer in peers:
        pl.semaphore_signal(barrier, inc=1, device_id=peer, device_id_type=MESH)
    pl.semaphore_wait(barrier, len(peers))


def others(stage, size):
    me, device = place(stage)
    return [device(lax.rem(me + step, size)) for step in range(1, size)]


def send(src, dst, send_sem, recv_sem, peer):
    copy = pltpu.make_async_remote_copy(
        src_ref=src,
        dst_ref=dst,
        send_sem=send_sem,
        recv_sem=recv_sem,
        device_id=peer,
        device_id_type=MESH,
    )
    copy.start()
    return copy


def scatter_kernel(
    nrow, nchip, x_ref, y_ref, x_out, y_out, core_x, core_y, held, chip_in, sums, row_in, *sems
):
    core_send, core_recv, chip_send, chip_recv, row_send, row_recv = sems
    row, _ = place("row")
    chip, _ = place("chip")
    core, _ = place("core")
    rows, chips, cores = others("row", nrow), others("chip", nchip), others("core", 2)
    enter(rows + chips + cores)
    count = x_ref.shape[-2]
    pieces = [(step, sup) for step in [*range(1, nrow), 0] for sup in range(NSUP)]
    owners = [lax.rem(row + step, nrow) for step, _ in pieces]
    from_core = []
    for at, (_, sup) in enumerate(pieces):
        to = owners[at]
        from_core.append(
            [
                send(
                    src.at[sup, to, :, 1 - core],
                    dst.at[at],
                    core_send.at[at, which],
                    core_recv.at[at, which],
                    cores[0],
                )
                for which, (src, dst) in enumerate(((x_ref, core_x), (y_ref, core_y)))
            ]
        )
    from_chips = []
    from_rows = []

    def finish(at):
        step, sup = pieces[at]
        for copy in from_chips[at]:
            copy.wait_recv()
        total = held[at, chip]
        for near in range(nchip - 1):
            total += chip_in[at, near]
        sums[at] = total
        if step > 0:
            from_rows.append(
                send(
                    sums.at[at],
                    row_in.at[at],
                    row_send.at[at],
                    row_recv.at[at],
                    rows[step - 1],
                )
            )

    for at, (_, sup) in enumerate(pieces):
        for copy in from_core[at]:
            copy.wait_recv()
        held[at, :, :count] = x_ref[sup, owners[at], :, core] + core_x[at]
        held[at, :, count:] = y_ref[sup, owners[at], :, core] + core_y[at]
        from_chips.append(
            [
                send(
                    held.at[at, lax.rem(chip + near + 1, nchip)],
                    chip_in.at[at, near],
                    chip_send.at[at, near],
                    chip_recv.at[at, near],
                    peer,
                )
                for near, peer in enumerate(chips)
            ]
        )
        if at >= 2:
            finish(at - 2)
    finish(len(pieces) - 2)
    finish(len(pieces) - 1)
    for copy in from_rows:
        copy.wait_recv()
    for sup in range(NSUP):
        total = sums[(nrow - 1) * NSUP + sup]
        for step in range(nrow - 1):
            total += row_in[step * NSUP + sup]
        x_out[sup] = total[:count]
        y_out[sup] = total[count:]
    for group in from_core + from_chips + [from_rows]:
        for copy in group:
            copy.wait_send()


def scatter(x, y, nrow, nchip, collective_id):
    count, part = x.shape[-2], y.shape[-2]
    n = nrow * NSUP
    f32 = jnp.float32
    vmem = pl.BlockSpec(memory_space=pltpu.VMEM)
    core, chip, row = (n, 2), (n, nchip - 1), (n - NSUP,)
    return pl.pallas_call(
        functools.partial(scatter_kernel, nrow, nchip),
        out_shape=[
            jax.ShapeDtypeStruct((NSUP, count, W), f32),
            jax.ShapeDtypeStruct((NSUP, part, W), f32),
        ],
        in_specs=[vmem, vmem],
        out_specs=[vmem, vmem],
        scratch_shapes=[
            pltpu.VMEM((n, nchip, count, W), f32),
            pltpu.VMEM((n, nchip, part, W), f32),
            pltpu.VMEM((n, nchip, count + part, W), f32),
            pltpu.VMEM((n, nchip - 1, count + part, W), f32),
            pltpu.VMEM((n, count + part, W), f32),
            pltpu.VMEM((n - NSUP, count + part, W), f32),
            *(pltpu.SemaphoreType.DMA(s) for s in (core, core, chip, chip, row, row)),
        ],
        compiler_params=pltpu.CompilerParams(
            collective_id=collective_id,
            has_side_effects=True,
            vmem_limit_bytes=44 * 1024 * 1024,
        ),
    )(x, y)


def gather_kernel(nrow, nchip, known, x_ref, out_ref, *sems):
    row_send, row_recv, chip_send, chip_recv, core_send, core_recv = sems
    row, _ = place("row")
    chip, _ = place("chip")
    core, _ = place("core")
    rows, chips, cores = others("row", nrow), others("chip", nchip), others("core", 2)
    enter(rows + chips + cores)
    started = []

    def forward(*args):
        started.append(send(*args))
        return started[-1]

    mine = out_ref.at[:, row, chip, core]
    from_rows = [
        forward(x_ref, mine, row_send.at[step], row_recv.at[step], peer)
        for step, peer in enumerate(rows)
    ]
    from_chips = []
    last = []
    for near in range(1 if known else 0, nrow):
        src = x_ref
        slot = mine
        if near > 0:
            from_rows[near - 1].wait_recv()
            slot = out_ref.at[:, lax.rem(row - near + nrow, nrow), chip, core]
            src = slot
        for step, peer in enumerate(chips):
            from_chips.append(
                (
                    near,
                    step + 1,
                    forward(src, slot, chip_send.at[step, near], chip_recv.at[step, near], peer),
                )
            )
        last.append(forward(src, slot, core_send.at[0, near], core_recv.at[0, near], cores[0]))
    for near, step, copy in from_chips:
        copy.wait_recv()
        slot = out_ref.at[
            :, lax.rem(row - near + nrow, nrow), lax.rem(chip - step + nchip, nchip), core
        ]
        last.append(
            forward(slot, slot, core_send.at[step, near], core_recv.at[step, near], cores[0])
        )
    for copy in last:
        copy.wait_recv()
    for copy in started:
        copy.wait_send()


def gather(x, nrow, nchip, collective_id, plane=None):
    shape = (x.shape[0], nrow, nchip, 2) + x.shape[1:]
    row, chip, core = ((nrow - 1,), (nchip - 1, nrow), (nchip, nrow))
    full = pl.pallas_call(
        functools.partial(gather_kernel, nrow, nchip, plane is not None),
        out_shape=jax.ShapeDtypeStruct(shape, x.dtype),
        in_specs=[pl.BlockSpec(memory_space=pl.ANY)],
        out_specs=pl.BlockSpec(memory_space=pl.ANY),
        scratch_shapes=[
            pltpu.SemaphoreType.DMA(n) for n in (row, row, chip, chip, core, core)
        ],
        compiler_params=pltpu.CompilerParams(
            collective_id=collective_id, has_side_effects=True
        ),
    )(x)
    if plane is not None:
        plane = plane.reshape(x.shape[0], 1, nchip, 2, *x.shape[1:])
        return lax.dynamic_update_slice(full, plane, (0, place("row")[0], 0, 0, 0, 0))
    where = (0, place("row")[0], place("chip")[0], place("core")[0], 0, 0)
    return lax.dynamic_update_slice(full, x[:, None, None, None], where)


def dot(a, b, contract):
    def split(x):
        high = x.astype(jnp.bfloat16)
        return high, (x - high.astype(jnp.float32)).astype(jnp.bfloat16)

    def one(x, y):
        return lax.dot_general(
            x, y, ((contract, (0,)), ((), ())), preferred_element_type=jnp.float32
        )

    a_high, a_low = split(a)
    b_high, b_low = split(b)
    return one(a_low, b_high) + one(a_high, b_low) + one(a_high, b_high)


def product_kernel(rows_ref, cols_ref, *refs):
    *tiles, l_ref, p_ref, d_ref = refs
    sup, i = pl.program_id(0), pl.program_id(1)
    row_hit = rows_ref[sup, i] >= 0

    @pl.when(i == 0)
    def _():
        d_ref[...] = jnp.zeros_like(d_ref)

    p_ref[...] = jnp.zeros_like(p_ref)

    @pl.when(row_hit)
    def _():
        for j, a_ref in enumerate(tiles):

            @pl.when(cols_ref[sup, j] >= 0)
            def _():
                p_ref[0] -= dot(a_ref[...], l_ref[0, j * TILE:(j + 1) * TILE, :], (1,))

        block = l_ref[0, pl.ds(pl.multiple_of(i * TILE, TILE), TILE), :]
        d_ref[0] += dot(block, p_ref[0], (0,))


def products(rows, cols, ancestor, lfull):
    def tile(j):
        def index(sup, i, rows_ref, cols_ref):
            row, col = rows_ref[sup, i], cols_ref[sup, j]
            hit = (row >= 0) & (col >= 0)
            return jnp.where(hit, row, 0), jnp.where(hit, col, 0)

        return pl.BlockSpec((TILE, TILE), index)

    total = lfull.shape[1]
    return pl.pallas_call(
        product_kernel,
        out_shape=(
            jax.ShapeDtypeStruct((NSUP, total, W), jnp.float32),
            jax.ShapeDtypeStruct((NSUP, W, W), jnp.float32),
        ),
        grid_spec=pltpu.PrefetchScalarGridSpec(
            num_scalar_prefetch=2,
            grid=(NSUP, NS),
            in_specs=[tile(j) for j in range(NS)]
            + [pl.BlockSpec((1, total, W), lambda sup, i, *_: (sup, 0, 0))],
            out_specs=[
                pl.BlockSpec((1, TILE, W), lambda sup, i, *_: (sup, i, 0)),
                pl.BlockSpec((1, W, W), lambda sup, i, *_: (sup, 0, 0)),
            ],
        ),
        compiler_params=pltpu.CompilerParams(vmem_limit_bytes=40 * 1024 * 1024),
    )(rows, cols, *[ancestor] * NS, lfull)


ROW_TILES = 16
COL_TILES = 8
UNIT = 16
ORDER = (3, 1, 2, 0)


def flip(value, bit):
    return value + bit - 2 * bit * lax.rem(lax.div(value, bit), 2)


def split(x):
    high = x.astype(jnp.bfloat16)
    return high, (x - high.astype(jnp.float32)).astype(jnp.bfloat16)


def dot3(a, b, contract):
    def one(x, y):
        return lax.dot_general(
            x, y, ((contract, (0,)), ((), ())), preferred_element_type=jnp.float32
        )

    (a_high, a_low), (b_high, b_low) = a, b
    return one(a_low, b_high) + one(a_high, b_low) + one(a_high, b_high)


def fused_kernel(rcap, ccap, *refs):
    t_ref, a_ref, l_ref, d_ref, off_ref, diag_ref, a_buf, b_high, b_low, tab, dinv = refs[:11]
    local_sem, send_sem, recv_sem, z_send, z_recv = refs[-5:]
    per_sup = refs[11:-5]
    groups = [per_sup[i * NSUP:(i + 1) * NSUP] for i in range(len(per_sup) // NSUP)]
    l_buf, p_buf, core_in, held, chip_in, mid_buf, total, d_buf, d_core, d_sum, d_in, e_buf, e_in, f_buf = groups
    row = lax.axis_index("prow")
    col = lax.axis_index("pcol")
    core = lax.rem(col, 2)
    chip = lax.div(col, 2)
    rows = [row, flip(row, 1), flip(row, 2), flip(flip(row, 1), 2)]
    chips = [chip, flip(chip, 1), flip(chip, 2), flip(flip(chip, 1), 2)]
    sibling = (row, chip * 2 + 1 - core)

    def on_row(s):
        return rows[s], col

    def on_chip(d):
        return row, chips[d] * 2 + core

    def across(d):
        return row, chips[d] * 2 + 1 - core

    started = []

    def send(src, dst, peer):
        at = len(started)
        copy = pltpu.make_async_remote_copy(
            src_ref=src,
            dst_ref=dst,
            send_sem=send_sem.at[at],
            recv_sem=recv_sem.at[at],
            device_id=peer,
            device_id_type=MESH,
        )
        copy.start()
        started.append(copy)
        return copy

    local = []

    def fetch(src, dst):
        copy = pltpu.make_async_copy(src, dst, local_sem.at[len(local)])
        copy.start()
        local.append(copy)
        return copy

    quarter = l_ref.shape[1]
    half = quarter // 2
    own_l = [
        [
            fetch(l_ref.at[sup, :, :, :, w * 128:(w + 1) * 128],
                  l_buf[sup].at[w, pl.ds(row * quarter, quarter)])
            for w in range(4)
        ]
        for sup in range(NSUP)
    ]
    own_a = [
        fetch(a_ref.at[:, :, j * TILE:(j + 1) * TILE], a_buf.at[j]) for j in range(COL_TILES)
    ]
    d_rows = 256 * core + 64 * row
    lanes = pl.ds(pl.multiple_of(chip * 128, 128), 128)
    own_d = fetch(d_ref.at[:, pl.ds(pl.multiple_of(d_rows, 64), 64), lanes], dinv)

    peers = [on_row(s) for s in (1, 2, 3)] + [on_chip(d) for d in (1, 2, 3)]
    peers += [sibling] + [across(d) for d in (1, 2, 3)]
    enter(peers)

    middle = lax.div(row * (3 - row), 2)
    sources = [
        rows[1],
        rows[2] + middle * (rows[3] - rows[2]),
        rows[3] + middle * (rows[2] - rows[3]),
    ]

    def piece(sup, source, d, begin=0, size=None):
        size = half if size is None else size
        return l_buf[sup].at[chips[d], pl.ds(source * quarter + core * half + begin, size)]

    def z_copy(sup, slot, src, dst, which, s):
        return pltpu.make_async_remote_copy(
            src_ref=src,
            dst_ref=dst,
            send_sem=z_send.at[sup, which],
            recv_sem=z_recv.at[sup, slot],
            device_id=on_row(s),
            device_id_type=MESH,
        )

    def z_own(sup, slot, which, s):
        return z_copy(
            sup, slot, l_ref.at[sup, pl.ds(core * half, half), :, :, lanes],
            piece(sup, row, 0), which, s)

    def z_pass(sup, slot, which):
        block = piece(sup, sources[slot], 0)
        return z_copy(sup, slot, block, block, which, 1)

    def send_rows(sup):
        z_own(sup, 0, 0, 1).start()

        @pl.when(middle == 1)
        def _():
            z_own(sup, 1, 1, 3).start()

        @pl.when(middle == 0)
        def _():
            z_own(sup, 2, 1, 2).start()

    from_x, from_y, from_far, from_sib = ([[] for _ in range(NSUP)] for _ in range(4))

    def spread_row(sup, slot):
        z_own(sup, slot, 0, 1).wait_recv()
        if slot > 0:
            @pl.when(middle == 1)
            def _():
                z_pass(sup, slot, slot + 1).start()

        block = piece(sup, sources[slot], 0)
        from_x[sup].append(send(block, block, on_chip(1)))
        from_y[sup].append(send(block, block, on_chip(2)))
        from_sib[sup].append(send(block, block, sibling))

    def spread_chips(sup):
        part = half // 2
        for slot, source in enumerate(sources):
            from_x[sup][slot].wait_recv()
            block = piece(sup, source, 1, 0, part)
            from_far[sup].append((source, 0, send(block, block, on_chip(2))))
            from_y[sup][slot].wait_recv()
            block = piece(sup, source, 2, part, part)
            from_far[sup].append((source, part, send(block, block, on_chip(1))))
            for d in (1, 2):
                block = piece(sup, source, d)
                from_sib[sup].append(send(block, block, sibling))

    def finish_l(sup):
        part = half // 2
        for source, begin, copy in from_far[sup]:
            copy.wait_recv()
            block = piece(sup, source, 3, begin, part)
            from_sib[sup].append(send(block, block, sibling))
        for copy in from_sib[sup]:
            copy.wait_recv()
        for copy in own_l[sup]:
            copy.wait()

    def finish_rows(sup):
        z_own(sup, 0, 0, 1).wait_send()
        z_own(sup, 1, 1, 1).wait_send()

        @pl.when(middle == 1)
        def _():
            for slot in (1, 2):
                z_pass(sup, slot, slot + 1).wait_send()

    width = 2 * rcap + 2 * NS + 3 * ccap

    def make_table(sup):
        tiles = [t_ref[sup, k] for k in range(NS)]

        def ranked(base, extent, cap):
            seen = jnp.int32(0)
            found = []
            for k in range(NS):
                at = tiles[k] - base
                hit = ((at >= 0) & (at < extent)).astype(jnp.int32)
                found.append((at, hit, seen))
                seen = seen + hit
            slots = []
            for s in range(cap):
                tile, pos, valid = jnp.int32(0), jnp.int32(0), jnp.int32(0)
                for k, (at, hit, rank) in enumerate(found):
                    here = hit * (rank == s).astype(jnp.int32)
                    tile = tile + here * at
                    pos = pos + here * k
                    valid = valid + here
                slots.append((tile, pos, valid))
            return slots, found

        slots, found = ranked(row * ROW_TILES, ROW_TILES, rcap)
        base = sup * width
        for s, (tile, pos, valid) in enumerate(slots):
            tab[base + s] = tile + (valid - 1) * ROW_TILES
            tab[base + rcap + s] = pos
        base += 2 * rcap
        for k, (_, hit, rank) in enumerate(found):
            tab[base + k] = hit
            tab[base + NS + k] = jnp.minimum(rank, rcap - 1)
        base += 2 * NS
        slots, _ = ranked(col * COL_TILES, COL_TILES, ccap)
        for s, (tile, pos, valid) in enumerate(slots):
            tab[base + s] = tile
            tab[base + ccap + s] = pos
            tab[base + 2 * ccap + s] = valid

    from_core = [[] for _ in range(NSUP)]

    def product(sup):
        base = sup * width
        cols = base + 2 * rcap + 2 * NS
        for t in range(ccap):
            pos = tab[cols + ccap + t]
            for w in range(4):
                block = l_buf[sup][w, pl.ds(pos * UNIT, UNIT)].reshape(TILE, 128)
                high, low = split(block)
                b_high[t * TILE:(t + 1) * TILE, w * 128:(w + 1) * 128] = high
                b_low[t * TILE:(t + 1) * TILE, w * 128:(w + 1) * 128] = low

        @pl.loop(0, rcap)
        def _(s):
            at = tab[base + s]
            tiles = []
            for t in range(ccap):
                hit = (at >= 0) & (tab[cols + 2 * ccap + t] > 0)
                block = a_buf[tab[cols + t], jnp.maximum(at, 0)]
                tiles.append(jnp.where(hit, block, 0.0))
            a = split(jnp.concatenate(tiles, axis=1))
            result = dot3(a, (b_high[...], b_low[...]), (1,))
            for w in range(4):
                block = result[:, w * 128:(w + 1) * 128].reshape(UNIT, 2, 8, 128)
                p_buf[sup][0, w, s] = block[:, 0]
                p_buf[sup][1, w, s] = block[:, 1]

        for d in ORDER:
            from_core[sup].append(
                send(p_buf[sup].at[1 - core, chips[d]], core_in[sup].at[chips[d]], sibling)
            )

    from_chips = [[] for _ in range(NSUP)]

    parts = (slice(0, UNIT // 2), slice(UNIT // 2, UNIT))

    def reduce_send(sup):
        for at, d in enumerate(ORDER):
            from_core[sup][at].wait_recv()
            w = chips[d]
            held[sup][w] = p_buf[sup][core, w] + core_in[sup][w]
            for which, near in enumerate((1, 2)):
                if d in (near, 3):
                    src = held[sup].at[w, :, parts[which]]
                    to = chip_in[sup].at[2 * which + (d == 3)]
                    from_chips[sup].append((2 * which + (d == 3), send(src, to, on_chip(near))))

    def reduce_pass(sup):
        first = dict(from_chips[sup])
        for which, near in enumerate((1, 2)):
            first[2 * which + 1].wait_recv()
            other = 3 - near
            block = held[sup][chips[other], :, parts[which]]
            mid_buf[sup][which] = block + chip_in[sup][2 * which + 1]
            from_chips[sup].append(
                (4 + which, send(mid_buf[sup].at[which], chip_in[sup].at[4 + which], on_chip(other)))
            )

    from_d = [None] * NSUP

    def reduce_finish(sup):
        for at, copy in from_chips[sup]:
            if at in (0, 2, 4, 5):
                copy.wait_recv()
        for which in range(2):
            block = held[sup][chip, :, parts[which]] + chip_in[sup][2 * which]
            total[sup][:, parts[which]] = block + chip_in[sup][4 + which]
        base = sup * width
        picked = []
        for s in range(rcap):
            pos = tab[base + rcap + s]
            picked.append(
                jnp.concatenate(
                    [
                        l_buf[sup][w, pl.ds(pos * UNIT, UNIT), core].reshape(128, 128)
                        for w in range(4)
                    ],
                    axis=1,
                )
            )
        left = split(jnp.concatenate(picked, axis=0))
        right = split(total[sup][...].reshape(rcap * 128, 128))
        d_buf[sup][...] = dot3(left, right, (0,)).reshape(2, 256, 128)
        from_d[sup] = send(d_buf[sup].at[1 - core], d_core[sup], sibling)

    from_e = [[] for _ in range(NSUP)]

    def listed(sup, to, put):
        base = sup * width + 2 * rcap
        for j in range(3):
            unit = 3 * to + j
            k = lax.div(unit, 2)
            begin = pl.multiple_of(8 * lax.rem(unit, 2), 8)
            block = total[sup][tab[base + NS + k], pl.ds(begin, 8)]
            put(j, jnp.where(tab[base + k] > 0, block, 0.0))

    def exchange(sup):
        for s in (1, 2, 3):
            def put(j, block):
                e_buf[sup][s - 1, 8 * j:8 * j + 8] = block

            listed(sup, rows[s], put)
            from_e[sup].append(
                send(e_buf[sup].at[s - 1], e_in[sup].at[s - 1], on_row(s))
            )

    from_dr = [[] for _ in range(NSUP)]

    def diag_rows(sup):
        from_d[sup].wait_recv()
        d_sum[sup][...] = (d_buf[sup][core] + d_core[sup][...]).reshape(4, 64, 128)
        for s in (1, 2, 3):
            from_dr[sup].append(
                send(d_sum[sup].at[rows[s]], d_in[sup].at[s - 1], on_row(s))
            )

    from_g = [[] for _ in range(NSUP)]

    def diag_piece(sup):
        for copy in from_dr[sup]:
            copy.wait_recv()
        mine = diag_ref.at[sup, pl.ds(pl.multiple_of(d_rows, 64), 64), lanes]
        value = d_sum[sup][row] + d_in[sup][0] + d_in[sup][1] + d_in[sup][2]
        mine[...] = dinv[sup] + value
        for s in (1, 2, 3):
            from_g[sup].append(send(mine, mine, on_row(s)))

    from_gc = [[] for _ in range(NSUP)]
    from_gs = [[] for _ in range(NSUP)]

    def diag_block(sup, d):
        at = pl.ds(pl.multiple_of(chips[d] * 128, 128), 128)
        return diag_ref.at[sup, pl.ds(pl.multiple_of(256 * core, 256), 256), at]

    def diag_chips(sup):
        for copy in from_g[sup]:
            copy.wait_recv()
        block = diag_block(sup, 0)
        for d in (1, 2, 3):
            from_gc[sup].append(send(block, block, on_chip(d)))
        from_gs[sup].append(send(block, block, sibling))

    def diag_cores(sup):
        for d in (1, 2, 3):
            from_gc[sup][d - 1].wait_recv()
            block = diag_block(sup, d)
            from_gs[sup].append(send(block, block, sibling))

    from_o = [[] for _ in range(NSUP)]

    def owners(sup):
        for copy in from_e[sup]:
            copy.wait_recv()

        def put(j, block):
            at = slice(8 * j, 8 * j + 8)
            rest = e_in[sup][0, at] + e_in[sup][1, at] + e_in[sup][2, at]
            f_buf[sup][at] = -(block + rest)

        listed(sup, row, put)
        place_at = off_ref.at[sup, :, core, :, lanes]

        def share(to):
            return f_buf[sup].at[pl.ds(3 * to, 3)]

        for d in (1, 2, 3):
            for peer in (on_chip(d), across(d)):
                from_o[sup].append(send(share(peer[1]), place_at, peer))
        from_o[sup].append(send(share(sibling[1]), place_at, sibling))
        off_ref[sup, :, core, :, lanes] = f_buf[sup][pl.ds(3 * col, 3)]

    send_rows(0)
    for sup in range(NSUP):
        make_table(sup)
    spread_row(0, 0)
    send_rows(1)
    spread_row(0, 1)
    spread_row(0, 2)
    spread_chips(0)
    for slot in range(3):
        spread_row(1, slot)
    finish_l(0)
    for copy in own_a:
        copy.wait()
    product(0)
    spread_chips(1)
    reduce_send(0)
    finish_l(1)
    reduce_pass(0)
    product(1)
    reduce_finish(0)
    reduce_send(1)
    diag_rows(0)
    exchange(0)
    reduce_pass(1)
    own_d.wait()
    diag_piece(0)
    reduce_finish(1)
    diag_rows(1)
    exchange(1)
    diag_chips(0)
    owners(0)
    diag_piece(1)
    diag_cores(0)
    diag_chips(1)
    owners(1)
    diag_cores(1)
    for sup in range(NSUP):
        finish_rows(sup)
    for group in from_gs + from_o:
        for copy in group:
            copy.wait_recv()
    for copy in started:
        copy.wait_send()


def fused(rcap, ccap, tile_lists, ancestor, l_scaled, diag_inv):
    f32 = jnp.float32
    total_rows = l_scaled.shape[1] * 4
    units = total_rows // UNIT
    view = l_scaled.reshape(NSUP, l_scaled.shape[1] // UNIT, 2, 8, W)
    any_space = pl.BlockSpec(memory_space=pl.ANY)
    vmem = pl.BlockSpec(memory_space=pltpu.VMEM)
    block = (rcap, UNIT, 8, 128)
    per_sup = [
        (4, units, 2, 8, 128),
        (2, 4) + block,
        (4,) + block,
        (4,) + block,
        (6, rcap, UNIT // 2, 8, 128),
        (2, rcap, UNIT // 2, 8, 128),
        block,
        (2, 256, 128),
        (256, 128),
        (4, 64, 128),
        (3, 64, 128),
        (3, 24, 8, 128),
        (3, 24, 8, 128),
        (24, 8, 128),
    ]
    scratch = [
        pltpu.VMEM((COL_TILES, ROW_TILES, TILE, TILE), f32),
        pltpu.VMEM((ccap * TILE, W), jnp.bfloat16),
        pltpu.VMEM((ccap * TILE, W), jnp.bfloat16),
        pltpu.SMEM((NSUP * (2 * rcap + 2 * NS + 3 * ccap),), jnp.int32),
        pltpu.VMEM((NSUP, 64, 128), f32),
    ]
    for shape in per_sup:
        scratch += [pltpu.VMEM(shape, f32)] * NSUP
    sends = NSUP * (6 + 6 + 15 + 4 + 6 + 1 + 3 + 3 + 3 + 3 + 4 + 7)
    scratch += [
        pltpu.SemaphoreType.DMA((4 * NSUP + COL_TILES + 1,)),
        pltpu.SemaphoreType.DMA((sends,)),
        pltpu.SemaphoreType.DMA((sends,)),
        pltpu.SemaphoreType.DMA((NSUP, 4)),
        pltpu.SemaphoreType.DMA((NSUP, 3)),
    ]
    off, diag = pl.pallas_call(
        functools.partial(fused_kernel, rcap, ccap),
        out_shape=[
            jax.ShapeDtypeStruct((NSUP, 3, 2, 8, W), f32),
            jax.ShapeDtypeStruct((NSUP, W, W), f32),
        ],
        in_specs=[pl.BlockSpec(memory_space=pltpu.SMEM), any_space, any_space, any_space],
        out_specs=[vmem, vmem],
        scratch_shapes=scratch,
        compiler_params=pltpu.CompilerParams(
            collective_id=6 + rcap,
            has_side_effects=True,
            vmem_limit_bytes=60 * 1024 * 1024,
        ),
    )(tile_lists, ancestor.reshape(ROW_TILES, TILE, -1), view, diag_inv)
    return off.reshape(NSUP, 48, W), diag


def fits(tile_lists, rcap, ccap):
    counts = []
    for extent, cap in ((ROW_TILES, rcap), (COL_TILES, ccap)):
        for begin in range(0, ROW_TILES * 4, extent):
            counts.append((begin, begin + extent, cap))
    begin, end, cap = (jnp.array(x, jnp.int32)[:, None] for x in zip(*counts))
    tiles = tile_lists[:, None, :]
    held = ((tiles >= begin) & (tiles < end)).astype(jnp.int32)
    return jnp.all(jnp.sum(held, axis=2) <= cap[:, 0])


def per_device(nrow, ncol, ancestor_inv, l_scaled, diag_inv, tile_lists):
    if (nrow, ncol) == (4, 8):
        args = (tile_lists, ancestor_inv, l_scaled, diag_inv)
        return lax.cond(
            fits(tile_lists, 4, 3),
            functools.partial(fused, 4, 3),
            functools.partial(fused, NS - 1, NS - 1),
            *args,
        )
    return stepwise(nrow, ncol, ancestor_inv, l_scaled, diag_inv, tile_lists)


def stepwise(nrow, ncol, ancestor_inv, l_scaled, diag_inv, tile_lists):
    nchip = ncol // 2
    tile_rows = ancestor_inv.shape[0] // TILE
    tile_cols = ancestor_inv.shape[1] // TILE
    row_pos = lax.axis_index("prow")
    col_pos = lax.axis_index("pcol")
    count = l_scaled.shape[1] // ncol
    part = W // (nrow * ncol)
    total = l_scaled.shape[1] * nrow

    share = lax.dynamic_slice_in_dim(l_scaled, col_pos * count, count, 1)
    lfull = gather(share, nrow, nchip, 1, l_scaled).reshape(NSUP, total, W)

    rows = tile_lists - row_pos * tile_rows
    rows = jnp.where((rows >= 0) & (rows < tile_rows), rows, -1)
    cols = tile_lists - col_pos * tile_cols
    cols = jnp.where((cols >= 0) & (cols < tile_cols), cols, -1)
    rows = jnp.where(jnp.max(cols, axis=1, keepdims=True) >= 0, rows, -1)
    partial, terms = products(rows, cols, ancestor_inv, lfull)

    mine, term = scatter(
        partial.reshape(NSUP, nrow, nchip, 2, count, W),
        terms.reshape(NSUP, nrow, nchip, 2, part, W),
        nrow,
        nchip,
        2,
    )
    diag = gather(term, nrow, nchip, 5).reshape(NSUP, W, W)
    return mine, diag_inv - diag


def solution(mesh):
    placed = (P("prow", "pcol"), P(None, "prow", None), P(), P())
    return jax.shard_map(
        functools.partial(per_device, mesh.shape["prow"], mesh.shape["pcol"]),
        mesh=mesh,
        in_specs=placed,
        out_specs=(P(None, ("prow", "pcol"), None), P()),
        check_vma=False,
    )
```

```python
import functools

import jax
import jax.numpy as jnp
from jax import lax
from jax.experimental import pallas as pl
from jax.experimental.pallas import tpu as pltpu
from jax.sharding import PartitionSpec as P

TILE = 256
W = 512
NS = 6
NSUP = 2
MESH = pl.DeviceIdType.MESH


def place(stage):
    row = lax.axis_index("prow")
    col = lax.axis_index("pcol")
    core = lax.rem(col, 2)
    chip = col // 2
    if stage == "row":
        return row, lambda m: (m, col)
    if stage == "chip":
        return chip, lambda m: (row, m * 2 + core)
    return core, lambda m: (row, chip * 2 + m)


def enter(peers):
    barrier = pltpu.get_barrier_semaphore()
    for peer in peers:
        pl.semaphore_signal(barrier, inc=1, device_id=peer, device_id_type=MESH)
    pl.semaphore_wait(barrier, len(peers))


def others(stage, size):
    me, device = place(stage)
    return [device(lax.rem(me + step, size)) for step in range(1, size)]


def send(src, dst, send_sem, recv_sem, peer):
    copy = pltpu.make_async_remote_copy(
        src_ref=src,
        dst_ref=dst,
        send_sem=send_sem,
        recv_sem=recv_sem,
        device_id=peer,
        device_id_type=MESH,
    )
    copy.start()
    return copy


def scatter_kernel(
    nrow, nchip, x_ref, y_ref, x_out, y_out, core_x, core_y, held, chip_in, sums, row_in, *sems
):
    core_send, core_recv, chip_send, chip_recv, row_send, row_recv = sems
    row, _ = place("row")
    chip, _ = place("chip")
    core, _ = place("core")
    rows, chips, cores = others("row", nrow), others("chip", nchip), others("core", 2)
    enter(rows + chips + cores)
    count = x_ref.shape[-2]
    pieces = [(step, sup) for step in [*range(1, nrow), 0] for sup in range(NSUP)]
    owners = [lax.rem(row + step, nrow) for step, _ in pieces]
    from_core = []
    for at, (_, sup) in enumerate(pieces):
        to = owners[at]
        from_core.append(
            [
                send(
                    src.at[sup, to, :, 1 - core],
                    dst.at[at],
                    core_send.at[at, which],
                    core_recv.at[at, which],
                    cores[0],
                )
                for which, (src, dst) in enumerate(((x_ref, core_x), (y_ref, core_y)))
            ]
        )
    from_chips = []
    from_rows = []

    def finish(at):
        step, sup = pieces[at]
        for copy in from_chips[at]:
            copy.wait_recv()
        total = held[at, chip]
        for near in range(nchip - 1):
            total += chip_in[at, near]
        sums[at] = total
        if step > 0:
            from_rows.append(
                send(
                    sums.at[at],
                    row_in.at[at],
                    row_send.at[at],
                    row_recv.at[at],
                    rows[step - 1],
                )
            )

    for at, (_, sup) in enumerate(pieces):
        for copy in from_core[at]:
            copy.wait_recv()
        held[at, :, :count] = x_ref[sup, owners[at], :, core] + core_x[at]
        held[at, :, count:] = y_ref[sup, owners[at], :, core] + core_y[at]
        from_chips.append(
            [
                send(
                    held.at[at, lax.rem(chip + near + 1, nchip)],
                    chip_in.at[at, near],
                    chip_send.at[at, near],
                    chip_recv.at[at, near],
                    peer,
                )
                for near, peer in enumerate(chips)
            ]
        )
        if at >= 2:
            finish(at - 2)
    finish(len(pieces) - 2)
    finish(len(pieces) - 1)
    for copy in from_rows:
        copy.wait_recv()
    for sup in range(NSUP):
        total = sums[(nrow - 1) * NSUP + sup]
        for step in range(nrow - 1):
            total += row_in[step * NSUP + sup]
        x_out[sup] = total[:count]
        y_out[sup] = total[count:]
    for group in from_core + from_chips + [from_rows]:
        for copy in group:
            copy.wait_send()


def scatter(x, y, nrow, nchip, collective_id):
    count, part = x.shape[-2], y.shape[-2]
    n = nrow * NSUP
    f32 = jnp.float32
    vmem = pl.BlockSpec(memory_space=pltpu.VMEM)
    core, chip, row = (n, 2), (n, nchip - 1), (n - NSUP,)
    return pl.pallas_call(
        functools.partial(scatter_kernel, nrow, nchip),
        out_shape=[
            jax.ShapeDtypeStruct((NSUP, count, W), f32),
            jax.ShapeDtypeStruct((NSUP, part, W), f32),
        ],
        in_specs=[vmem, vmem],
        out_specs=[vmem, vmem],
        scratch_shapes=[
            pltpu.VMEM((n, nchip, count, W), f32),
            pltpu.VMEM((n, nchip, part, W), f32),
            pltpu.VMEM((n, nchip, count + part, W), f32),
            pltpu.VMEM((n, nchip - 1, count + part, W), f32),
            pltpu.VMEM((n, count + part, W), f32),
            pltpu.VMEM((n - NSUP, count + part, W), f32),
            *(pltpu.SemaphoreType.DMA(s) for s in (core, core, chip, chip, row, row)),
        ],
        compiler_params=pltpu.CompilerParams(
            collective_id=collective_id,
            has_side_effects=True,
            vmem_limit_bytes=44 * 1024 * 1024,
        ),
    )(x, y)


def gather_kernel(nrow, nchip, known, x_ref, out_ref, *sems):
    row_send, row_recv, chip_send, chip_recv, core_send, core_recv = sems
    row, _ = place("row")
    chip, _ = place("chip")
    core, _ = place("core")
    rows, chips, cores = others("row", nrow), others("chip", nchip), others("core", 2)
    enter(rows + chips + cores)
    started = []

    def forward(*args):
        started.append(send(*args))
        return started[-1]

    mine = out_ref.at[:, row, chip, core]
    from_rows = [
        forward(x_ref, mine, row_send.at[step], row_recv.at[step], peer)
        for step, peer in enumerate(rows)
    ]
    from_chips = []
    last = []
    for near in range(1 if known else 0, nrow):
        src = x_ref
        slot = mine
        if near > 0:
            from_rows[near - 1].wait_recv()
            slot = out_ref.at[:, lax.rem(row - near + nrow, nrow), chip, core]
            src = slot
        for step, peer in enumerate(chips):
            from_chips.append(
                (
                    near,
                    step + 1,
                    forward(src, slot, chip_send.at[step, near], chip_recv.at[step, near], peer),
                )
            )
        last.append(forward(src, slot, core_send.at[0, near], core_recv.at[0, near], cores[0]))
    for near, step, copy in from_chips:
        copy.wait_recv()
        slot = out_ref.at[
            :, lax.rem(row - near + nrow, nrow), lax.rem(chip - step + nchip, nchip), core
        ]
        last.append(
            forward(slot, slot, core_send.at[step, near], core_recv.at[step, near], cores[0])
        )
    for copy in last:
        copy.wait_recv()
    for copy in started:
        copy.wait_send()


def gather(x, nrow, nchip, collective_id, plane=None):
    shape = (x.shape[0], nrow, nchip, 2) + x.shape[1:]
    row, chip, core = ((nrow - 1,), (nchip - 1, nrow), (nchip, nrow))
    full = pl.pallas_call(
        functools.partial(gather_kernel, nrow, nchip, plane is not None),
        out_shape=jax.ShapeDtypeStruct(shape, x.dtype),
        in_specs=[pl.BlockSpec(memory_space=pl.ANY)],
        out_specs=pl.BlockSpec(memory_space=pl.ANY),
        scratch_shapes=[
            pltpu.SemaphoreType.DMA(n) for n in (row, row, chip, chip, core, core)
        ],
        compiler_params=pltpu.CompilerParams(
            collective_id=collective_id, has_side_effects=True
        ),
    )(x)
    if plane is not None:
        plane = plane.reshape(x.shape[0], 1, nchip, 2, *x.shape[1:])
        return lax.dynamic_update_slice(full, plane, (0, place("row")[0], 0, 0, 0, 0))
    where = (0, place("row")[0], place("chip")[0], place("core")[0], 0, 0)
    return lax.dynamic_update_slice(full, x[:, None, None, None], where)


def dot(a, b, contract):
    def split(x):
        high = x.astype(jnp.bfloat16)
        return high, (x - high.astype(jnp.float32)).astype(jnp.bfloat16)

    def one(x, y):
        return lax.dot_general(
            x, y, ((contract, (0,)), ((), ())), preferred_element_type=jnp.float32
        )

    a_high, a_low = split(a)
    b_high, b_low = split(b)
    return one(a_low, b_high) + one(a_high, b_low) + one(a_high, b_high)


def product_kernel(rows_ref, cols_ref, *refs):
    *tiles, l_ref, p_ref, d_ref = refs
    sup, i = pl.program_id(0), pl.program_id(1)
    row_hit = rows_ref[sup, i] >= 0

    @pl.when(i == 0)
    def _():
        d_ref[...] = jnp.zeros_like(d_ref)

    p_ref[...] = jnp.zeros_like(p_ref)

    @pl.when(row_hit)
    def _():
        for j, a_ref in enumerate(tiles):

            @pl.when(cols_ref[sup, j] >= 0)
            def _():
                p_ref[0] -= dot(a_ref[...], l_ref[0, j * TILE:(j + 1) * TILE, :], (1,))

        block = l_ref[0, pl.ds(pl.multiple_of(i * TILE, TILE), TILE), :]
        d_ref[0] += dot(block, p_ref[0], (0,))


def products(rows, cols, ancestor, lfull):
    def tile(j):
        def index(sup, i, rows_ref, cols_ref):
            row, col = rows_ref[sup, i], cols_ref[sup, j]
            hit = (row >= 0) & (col >= 0)
            return jnp.where(hit, row, 0), jnp.where(hit, col, 0)

        return pl.BlockSpec((TILE, TILE), index)

    total = lfull.shape[1]
    return pl.pallas_call(
        product_kernel,
        out_shape=(
            jax.ShapeDtypeStruct((NSUP, total, W), jnp.float32),
            jax.ShapeDtypeStruct((NSUP, W, W), jnp.float32),
        ),
        grid_spec=pltpu.PrefetchScalarGridSpec(
            num_scalar_prefetch=2,
            grid=(NSUP, NS),
            in_specs=[tile(j) for j in range(NS)]
            + [pl.BlockSpec((1, total, W), lambda sup, i, *_: (sup, 0, 0))],
            out_specs=[
                pl.BlockSpec((1, TILE, W), lambda sup, i, *_: (sup, i, 0)),
                pl.BlockSpec((1, W, W), lambda sup, i, *_: (sup, 0, 0)),
            ],
        ),
        compiler_params=pltpu.CompilerParams(vmem_limit_bytes=40 * 1024 * 1024),
    )(rows, cols, *[ancestor] * NS, lfull)


ROW_TILES = 16
COL_TILES = 8
UNIT = 16
ORDER = (3, 1, 2, 0)


def flip(value, bit):
    return value + bit - 2 * bit * lax.rem(lax.div(value, bit), 2)


def split(x):
    high = x.astype(jnp.bfloat16)
    return high, (x - high.astype(jnp.float32)).astype(jnp.bfloat16)


def dot3(a, b, contract):
    def one(x, y):
        return lax.dot_general(
            x, y, ((contract, (0,)), ((), ())), preferred_element_type=jnp.float32
        )

    (a_high, a_low), (b_high, b_low) = a, b
    return one(a_low, b_high) + one(a_high, b_low) + one(a_high, b_high)


def fused_kernel(rcap, ccap, *refs):
    t_ref, a_ref, l_ref, d_ref, off_ref, diag_ref, a_buf, b_high, b_low, tab, dinv = refs[:11]
    local_sem, send_sem, recv_sem, z_send, z_recv = refs[-5:]
    per_sup = refs[11:-5]
    groups = [per_sup[i * NSUP:(i + 1) * NSUP] for i in range(len(per_sup) // NSUP)]
    l_buf, p_buf, core_in, held, chip_in, mid_buf, total, d_buf, d_core, d_sum, d_in, e_buf, e_in, f_buf = groups
    row = lax.axis_index("prow")
    col = lax.axis_index("pcol")
    core = lax.rem(col, 2)
    chip = lax.div(col, 2)
    rows = [row, flip(row, 1), flip(row, 2), flip(flip(row, 1), 2)]
    chips = [chip, flip(chip, 1), flip(chip, 2), flip(flip(chip, 1), 2)]
    sibling = (row, chip * 2 + 1 - core)

    def on_row(s):
        return rows[s], col

    def on_chip(d):
        return row, chips[d] * 2 + core

    def across(d):
        return row, chips[d] * 2 + 1 - core

    used = {}

    def send(src, dst, peer, group, shared=None):
        at = used.setdefault(shared or len(used), len(used))
        copy = pltpu.make_async_remote_copy(
            src_ref=src,
            dst_ref=dst,
            send_sem=send_sem.at[group],
            recv_sem=recv_sem.at[at],
            device_id=peer,
            device_id_type=MESH,
        )
        copy.start()
        return copy

    def gathered(shared, ref, group=0):
        return pltpu.make_async_remote_copy(
            src_ref=ref,
            dst_ref=ref,
            send_sem=send_sem.at[group],
            recv_sem=recv_sem.at[used[shared]],
            device_id=sibling,
            device_id_type=MESH,
        )

    local = []

    def fetch(src, dst):
        copy = pltpu.make_async_copy(src, dst, local_sem.at[len(local)])
        copy.start()
        local.append(copy)
        return copy

    quarter = l_ref.shape[1]
    half = quarter // 2
    own_l = [
        [
            fetch(l_ref.at[sup, :, :, :, w * 128:(w + 1) * 128],
                  l_buf[sup].at[w, pl.ds(row * quarter, quarter)])
            for w in range(4)
        ]
        for sup in range(NSUP)
    ]
    own_a = [
        fetch(a_ref.at[:, :, j * TILE:(j + 1) * TILE], a_buf.at[j]) for j in range(COL_TILES)
    ]
    d_rows = 256 * core + 64 * row
    lanes = pl.ds(pl.multiple_of(chip * 128, 128), 128)
    own_d = fetch(d_ref.at[:, pl.ds(pl.multiple_of(d_rows, 64), 64), lanes], dinv)

    peers = [on_row(s) for s in (1, 2, 3)] + [on_chip(d) for d in (1, 2, 3)]
    peers += [sibling] + [across(d) for d in (1, 2, 3)]
    enter(peers)

    middle = lax.div(row * (3 - row), 2)
    sources = [
        rows[1],
        rows[2] + middle * (rows[3] - rows[2]),
        rows[3] + middle * (rows[2] - rows[3]),
    ]

    def piece(sup, source, d, begin=0, size=None):
        size = half if size is None else size
        return l_buf[sup].at[chips[d], pl.ds(source * quarter + core * half + begin, size)]

    def z_copy(sup, slot, src, dst, which, s):
        return pltpu.make_async_remote_copy(
            src_ref=src,
            dst_ref=dst,
            send_sem=z_send.at[sup, which],
            recv_sem=z_recv.at[sup, slot],
            device_id=on_row(s),
            device_id_type=MESH,
        )

    def z_own(sup, slot, which, s):
        return z_copy(
            sup, slot, l_ref.at[sup, pl.ds(core * half, half), :, :, lanes],
            piece(sup, row, 0), which, s)

    def z_pass(sup, slot, which):
        block = piece(sup, sources[slot], 0)
        return z_copy(sup, slot, block, block, which, 1)

    def send_rows(sup):
        z_own(sup, 0, 0, 1).start()

        @pl.when(middle == 1)
        def _():
            z_own(sup, 1, 1, 3).start()

        @pl.when(middle == 0)
        def _():
            z_own(sup, 2, 1, 2).start()

    from_x, from_y, from_far = ([[] for _ in range(NSUP)] for _ in range(3))

    def spread_row(sup, slot):
        z_own(sup, slot, 0, 1).wait_recv()
        if slot > 0:
            @pl.when(middle == 1)
            def _():
                z_pass(sup, slot, slot + 1).start()

        block = piece(sup, sources[slot], 0)
        from_x[sup].append(send(block, block, on_chip(1), sup))
        from_y[sup].append(send(block, block, on_chip(2), sup))
        send(block, block, sibling, sup, ("l", sup))

    def spread_chips(sup):
        part = half // 2
        for slot, source in enumerate(sources):
            from_x[sup][slot].wait_recv()
            block = piece(sup, source, 1, 0, part)
            from_far[sup].append((source, 0, send(block, block, on_chip(2), sup)))
            from_y[sup][slot].wait_recv()
            block = piece(sup, source, 2, part, part)
            from_far[sup].append((source, part, send(block, block, on_chip(1), sup)))
            for d in (1, 2):
                block = piece(sup, source, d)
                send(block, block, sibling, sup, ("l", sup))

    def finish_l(sup):
        part = half // 2
        for source, begin, copy in from_far[sup]:
            copy.wait_recv()
            block = piece(sup, source, 3, begin, part)
            send(block, block, sibling, sup, ("l", sup))
        gathered(("l", sup), l_buf[sup].at[:, :3 * half]).wait_recv()
        for copy in own_l[sup]:
            copy.wait()

    def finish_rows(sup):
        z_own(sup, 0, 0, 1).wait_send()
        z_own(sup, 1, 1, 1).wait_send()

        @pl.when(middle == 1)
        def _():
            for slot in (1, 2):
                z_pass(sup, slot, slot + 1).wait_send()

    width = 2 * rcap + 2 * NS + 3 * ccap

    def make_table(sup):
        tiles = [t_ref[sup, k] for k in range(NS)]

        def ranked(base, extent, cap):
            seen = jnp.int32(0)
            found = []
            for k in range(NS):
                at = tiles[k] - base
                hit = ((at >= 0) & (at < extent)).astype(jnp.int32)
                found.append((at, hit, seen))
                seen = seen + hit
            slots = []
            for s in range(cap):
                tile, pos, valid = jnp.int32(0), jnp.int32(0), jnp.int32(0)
                for k, (at, hit, rank) in enumerate(found):
                    here = hit * (rank == s).astype(jnp.int32)
                    tile = tile + here * at
                    pos = pos + here * k
                    valid = valid + here
                slots.append((tile, pos, valid))
            return slots, found

        slots, found = ranked(row * ROW_TILES, ROW_TILES, rcap)
        base = sup * width
        for s, (tile, pos, valid) in enumerate(slots):
            tab[base + s] = tile + (valid - 1) * ROW_TILES
            tab[base + rcap + s] = pos
        base += 2 * rcap
        for k, (_, hit, rank) in enumerate(found):
            tab[base + k] = hit
            tab[base + NS + k] = jnp.minimum(rank, rcap - 1)
        base += 2 * NS
        slots, _ = ranked(col * COL_TILES, COL_TILES, ccap)
        for s, (tile, pos, valid) in enumerate(slots):
            tab[base + s] = tile
            tab[base + ccap + s] = pos
            tab[base + 2 * ccap + s] = valid

    from_core = [[] for _ in range(NSUP)]

    def product(sup):
        base = sup * width
        cols = base + 2 * rcap + 2 * NS
        for t in range(ccap):
            pos = tab[cols + ccap + t]
            for w in range(4):
                block = l_buf[sup][w, pl.ds(pos * UNIT, UNIT)].reshape(TILE, 128)
                high, low = split(block)
                b_high[t * TILE:(t + 1) * TILE, w * 128:(w + 1) * 128] = high
                b_low[t * TILE:(t + 1) * TILE, w * 128:(w + 1) * 128] = low

        @pl.loop(0, rcap)
        def _(s):
            at = tab[base + s]
            tiles = []
            for t in range(ccap):
                hit = (at >= 0) & (tab[cols + 2 * ccap + t] > 0)
                block = a_buf[tab[cols + t], jnp.maximum(at, 0)]
                tiles.append(jnp.where(hit, block, 0.0))
            a = split(jnp.concatenate(tiles, axis=1))
            result = dot3(a, (b_high[...], b_low[...]), (1,))
            for w in range(4):
                block = result[:, w * 128:(w + 1) * 128].reshape(UNIT, 2, 8, 128)
                p_buf[sup][0, w, s] = block[:, 0]
                p_buf[sup][1, w, s] = block[:, 1]

        for d in ORDER:
            from_core[sup].append(
                send(p_buf[sup].at[1 - core, chips[d]], core_in[sup].at[chips[d]], sibling, NSUP + sup)
            )

    from_chips = [[] for _ in range(NSUP)]

    parts = (slice(0, UNIT // 2), slice(UNIT // 2, UNIT))

    def reduce_send(sup):
        for at, d in enumerate(ORDER):
            from_core[sup][at].wait_recv()
            w = chips[d]
            held[sup][w] = p_buf[sup][core, w] + core_in[sup][w]
            for which, near in enumerate((1, 2)):
                if d in (near, 3):
                    src = held[sup].at[w, :, parts[which]]
                    to = chip_in[sup].at[2 * which + (d == 3)]
                    from_chips[sup].append((2 * which + (d == 3), send(src, to, on_chip(near), NSUP + sup)))

    def reduce_pass(sup):
        first = dict(from_chips[sup])
        for which, near in enumerate((1, 2)):
            first[2 * which + 1].wait_recv()
            other = 3 - near
            block = held[sup][chips[other], :, parts[which]]
            mid_buf[sup][which] = block + chip_in[sup][2 * which + 1]
            from_chips[sup].append(
                (
                    4 + which,
                    send(mid_buf[sup].at[which], chip_in[sup].at[4 + which], on_chip(other), NSUP + sup),
                )
            )

    from_d = [None] * NSUP

    def reduce_finish(sup):
        for at, copy in from_chips[sup]:
            if at in (0, 2, 4, 5):
                copy.wait_recv()
        for which in range(2):
            block = held[sup][chip, :, parts[which]] + chip_in[sup][2 * which]
            total[sup][:, parts[which]] = block + chip_in[sup][4 + which]
        base = sup * width
        picked = []
        for s in range(rcap):
            pos = tab[base + rcap + s]
            picked.append(
                jnp.concatenate(
                    [
                        l_buf[sup][w, pl.ds(pos * UNIT, UNIT), core].reshape(128, 128)
                        for w in range(4)
                    ],
                    axis=1,
                )
            )
        left = split(jnp.concatenate(picked, axis=0))
        right = split(total[sup][...].reshape(rcap * 128, 128))
        d_buf[sup][...] = dot3(left, right, (0,)).reshape(2, 256, 128)
        from_d[sup] = send(d_buf[sup].at[1 - core], d_core[sup], sibling, 2 * NSUP)

    def listed(sup, to, put):
        base = sup * width + 2 * rcap
        for j in range(3):
            unit = 3 * to + j
            k = lax.div(unit, 2)
            begin = pl.multiple_of(8 * lax.rem(unit, 2), 8)
            block = total[sup][tab[base + NS + k], pl.ds(begin, 8)]
            put(j, jnp.where(tab[base + k] > 0, block, 0.0))

    def exchange(sup):
        for s in (1, 2, 3):
            def put(j, block):
                e_buf[sup][s - 1, 8 * j:8 * j + 8] = block

            listed(sup, rows[s], put)
            send(e_buf[sup].at[s - 1], e_in[sup].at[s - 1], on_row(s), 2 * NSUP + 1, ("e", sup))

    def diag_rows(sup):
        from_d[sup].wait_recv()
        d_sum[sup][...] = (d_buf[sup][core] + d_core[sup][...]).reshape(4, 64, 128)
        for s in (1, 2, 3):
            send(d_sum[sup].at[rows[s]], d_in[sup].at[s - 1], on_row(s), 2 * NSUP, ("d", sup))

    def diag_piece(sup):
        gathered(("d", sup), d_in[sup]).wait_recv()
        mine = diag_ref.at[sup, pl.ds(pl.multiple_of(d_rows, 64), 64), lanes]
        value = d_sum[sup][row] + d_in[sup][0] + d_in[sup][1] + d_in[sup][2]
        mine[...] = dinv[sup] + value
        for s in (1, 2, 3):
            send(mine, mine, on_row(s), 2 * NSUP, ("g", sup))

    from_gc = [[] for _ in range(NSUP)]

    def diag_block(sup, d):
        at = pl.ds(pl.multiple_of(chips[d] * 128, 128), 128)
        return diag_ref.at[sup, pl.ds(pl.multiple_of(256 * core, 256), 256), at]

    def diag_chips(sup):
        gathered(("g", sup), d_in[sup]).wait_recv()
        block = diag_block(sup, 0)
        for d in (1, 2, 3):
            from_gc[sup].append(send(block, block, on_chip(d), 2 * NSUP))
        send(block, block, sibling, 2 * NSUP, "gs")

    def diag_cores(sup):
        for d in (1, 2, 3):
            from_gc[sup][d - 1].wait_recv()
            block = diag_block(sup, d)
            send(block, block, sibling, 2 * NSUP, "gs")

    def owners(sup):
        gathered(("e", sup), e_in[sup]).wait_recv()

        def put(j, block):
            at = slice(8 * j, 8 * j + 8)
            rest = e_in[sup][0, at] + e_in[sup][1, at] + e_in[sup][2, at]
            f_buf[sup][at] = -(block + rest)

        listed(sup, row, put)
        place_at = off_ref.at[sup, :, core, :, lanes]

        def share(to):
            return f_buf[sup].at[pl.ds(3 * to, 3)]

        for d in (1, 2, 3):
            for peer in (on_chip(d), across(d)):
                send(share(peer[1]), place_at, peer, 2 * NSUP + 1, "o")
        send(share(sibling[1]), place_at, sibling, 2 * NSUP + 1, "o")
        off_ref[sup, :, core, :, lanes] = f_buf[sup][pl.ds(3 * col, 3)]

    send_rows(0)
    for sup in range(NSUP):
        make_table(sup)
    spread_row(0, 0)
    send_rows(1)
    spread_row(0, 1)
    spread_row(0, 2)
    spread_chips(0)
    for slot in range(3):
        spread_row(1, slot)
    finish_l(0)
    for copy in own_a:
        copy.wait()
    product(0)
    spread_chips(1)
    reduce_send(0)
    finish_l(1)
    product(1)
    reduce_pass(0)
    reduce_send(1)
    reduce_finish(0)
    reduce_pass(1)
    diag_rows(0)
    exchange(0)
    reduce_finish(1)
    own_d.wait()
    diag_piece(0)
    diag_rows(1)
    exchange(1)
    diag_chips(0)
    diag_piece(1)
    owners(0)
    diag_chips(1)
    diag_cores(0)
    owners(1)
    diag_cores(1)
    for sup in range(NSUP):
        finish_rows(sup)
    gathered("gs", l_buf[0].at[:, :32]).wait_recv()
    gathered("o", l_buf[0].at[0, :21]).wait_recv()
    for sup in range(NSUP):
        gathered("o", l_buf[sup].at[:, :63], sup).wait_send()
        gathered("o", p_buf[sup].at[:, :, :, :14], NSUP + sup).wait_send()
    gathered("o", l_buf[0].at[:, :76], 2 * NSUP).wait_send()
    gathered("o", l_buf[0].at[0, :93], 2 * NSUP + 1).wait_send()


def fused(rcap, ccap, tile_lists, ancestor, l_scaled, diag_inv):
    f32 = jnp.float32
    total_rows = l_scaled.shape[1] * 4
    units = total_rows // UNIT
    view = l_scaled.reshape(NSUP, l_scaled.shape[1] // UNIT, 2, 8, W)
    any_space = pl.BlockSpec(memory_space=pl.ANY)
    vmem = pl.BlockSpec(memory_space=pltpu.VMEM)
    block = (rcap, UNIT, 8, 128)
    per_sup = [
        (4, units, 2, 8, 128),
        (2, 4) + block,
        (4,) + block,
        (4,) + block,
        (6, rcap, UNIT // 2, 8, 128),
        (2, rcap, UNIT // 2, 8, 128),
        block,
        (2, 256, 128),
        (256, 128),
        (4, 64, 128),
        (3, 64, 128),
        (3, 24, 8, 128),
        (3, 24, 8, 128),
        (24, 8, 128),
    ]
    scratch = [
        pltpu.VMEM((COL_TILES, ROW_TILES, TILE, TILE), f32),
        pltpu.VMEM((ccap * TILE, W), jnp.bfloat16),
        pltpu.VMEM((ccap * TILE, W), jnp.bfloat16),
        pltpu.SMEM((NSUP * (2 * rcap + 2 * NS + 3 * ccap),), jnp.int32),
        pltpu.VMEM((NSUP, 64, 128), f32),
    ]
    for shape in per_sup:
        scratch += [pltpu.VMEM(shape, f32)] * NSUP
    scratch += [
        pltpu.SemaphoreType.DMA((4 * NSUP + COL_TILES + 1,)),
        pltpu.SemaphoreType.DMA((2 * NSUP + 2,)),
        pltpu.SemaphoreType.DMA((NSUP * (6 + 6 + 1 + 4 + 6 + 1 + 1 + 1 + 1 + 3) + 2,)),
        pltpu.SemaphoreType.DMA((NSUP, 4)),
        pltpu.SemaphoreType.DMA((NSUP, 3)),
    ]
    off, diag = pl.pallas_call(
        functools.partial(fused_kernel, rcap, ccap),
        out_shape=[
            jax.ShapeDtypeStruct((NSUP, 3, 2, 8, W), f32),
            jax.ShapeDtypeStruct((NSUP, W, W), f32),
        ],
        in_specs=[pl.BlockSpec(memory_space=pltpu.SMEM), any_space, any_space, any_space],
        out_specs=[vmem, vmem],
        scratch_shapes=scratch,
        compiler_params=pltpu.CompilerParams(
            collective_id=6 + rcap,
            has_side_effects=True,
            vmem_limit_bytes=60 * 1024 * 1024,
        ),
    )(tile_lists, ancestor.reshape(ROW_TILES, TILE, -1), view, diag_inv)
    return off.reshape(NSUP, 48, W), diag


FOURS = 0x44444444


def packed_counts(tile_lists):
    field = 4 * jnp.arange(NSUP, dtype=jnp.int32)[:, None] + tile_lists // ROW_TILES
    return jnp.sum(jnp.left_shift(jnp.int32(1), 4 * field))


def per_device(nrow, ncol, ancestor_inv, l_scaled, diag_inv, tile_lists):
    if (nrow, ncol) == (4, 8):
        args = (tile_lists, ancestor_inv, l_scaled, diag_inv)
        counts = packed_counts(tile_lists)
        low, middle, top = (functools.partial(fused, cap, cap) for cap in (3, 4, NS - 1))

        def more(*rest):
            fives = counts & jnp.left_shift(counts, 2) & FOURS
            return lax.cond(fives == 0, middle, top, *rest)

        return lax.cond(counts & FOURS == 0, low, more, *args)
    return stepwise(nrow, ncol, ancestor_inv, l_scaled, diag_inv, tile_lists)


def stepwise(nrow, ncol, ancestor_inv, l_scaled, diag_inv, tile_lists):
    nchip = ncol // 2
    tile_rows = ancestor_inv.shape[0] // TILE
    tile_cols = ancestor_inv.shape[1] // TILE
    row_pos = lax.axis_index("prow")
    col_pos = lax.axis_index("pcol")
    count = l_scaled.shape[1] // ncol
    part = W // (nrow * ncol)
    total = l_scaled.shape[1] * nrow

    share = lax.dynamic_slice_in_dim(l_scaled, col_pos * count, count, 1)
    lfull = gather(share, nrow, nchip, 1, l_scaled).reshape(NSUP, total, W)

    rows = tile_lists - row_pos * tile_rows
    rows = jnp.where((rows >= 0) & (rows < tile_rows), rows, -1)
    cols = tile_lists - col_pos * tile_cols
    cols = jnp.where((cols >= 0) & (cols < tile_cols), cols, -1)
    rows = jnp.where(jnp.max(cols, axis=1, keepdims=True) >= 0, rows, -1)
    partial, terms = products(rows, cols, ancestor_inv, lfull)

    mine, term = scatter(
        partial.reshape(NSUP, nrow, nchip, 2, count, W),
        terms.reshape(NSUP, nrow, nchip, 2, part, W),
        nrow,
        nchip,
        2,
    )
    diag = gather(term, nrow, nchip, 5).reshape(NSUP, W, W)
    return mine, diag_inv - diag


def solution(mesh):
    placed = (P("prow", "pcol"), P(None, "prow", None), P(), P())
    return jax.shard_map(
        functools.partial(per_device, mesh.shape["prow"], mesh.shape["pcol"]),
        mesh=mesh,
        in_specs=placed,
        out_specs=(P(None, ("prow", "pcol"), None), P()),
        check_vma=False,
    )
```

```python
import functools

import jax
import jax.numpy as jnp
from jax import lax
from jax.experimental import pallas as pl
from jax.experimental.pallas import tpu as pltpu
from jax.sharding import PartitionSpec as P

TILE = 256
W = 512
NS = 6
NSUP = 2
MESH = pl.DeviceIdType.MESH


def place(stage):
    row = lax.axis_index("prow")
    col = lax.axis_index("pcol")
    core = lax.rem(col, 2)
    chip = col // 2
    if stage == "row":
        return row, lambda m: (m, col)
    if stage == "chip":
        return chip, lambda m: (row, m * 2 + core)
    return core, lambda m: (row, chip * 2 + m)


def enter(peers):
    barrier = pltpu.get_barrier_semaphore()
    for peer in peers:
        pl.semaphore_signal(barrier, inc=1, device_id=peer, device_id_type=MESH)
    pl.semaphore_wait(barrier, len(peers))


def others(stage, size):
    me, device = place(stage)
    return [device(lax.rem(me + step, size)) for step in range(1, size)]


def send(src, dst, send_sem, recv_sem, peer):
    copy = pltpu.make_async_remote_copy(
        src_ref=src,
        dst_ref=dst,
        send_sem=send_sem,
        recv_sem=recv_sem,
        device_id=peer,
        device_id_type=MESH,
    )
    copy.start()
    return copy


def scatter_kernel(
    nrow, nchip, x_ref, y_ref, x_out, y_out, core_x, core_y, held, chip_in, sums, row_in, *sems
):
    core_send, core_recv, chip_send, chip_recv, row_send, row_recv = sems
    row, _ = place("row")
    chip, _ = place("chip")
    core, _ = place("core")
    rows, chips, cores = others("row", nrow), others("chip", nchip), others("core", 2)
    enter(rows + chips + cores)
    count = x_ref.shape[-2]
    pieces = [(step, sup) for step in [*range(1, nrow), 0] for sup in range(NSUP)]
    owners = [lax.rem(row + step, nrow) for step, _ in pieces]
    from_core = []
    for at, (_, sup) in enumerate(pieces):
        to = owners[at]
        from_core.append(
            [
                send(
                    src.at[sup, to, :, 1 - core],
                    dst.at[at],
                    core_send.at[at, which],
                    core_recv.at[at, which],
                    cores[0],
                )
                for which, (src, dst) in enumerate(((x_ref, core_x), (y_ref, core_y)))
            ]
        )
    from_chips = []
    from_rows = []

    def finish(at):
        step, sup = pieces[at]
        for copy in from_chips[at]:
            copy.wait_recv()
        total = held[at, chip]
        for near in range(nchip - 1):
            total += chip_in[at, near]
        sums[at] = total
        if step > 0:
            from_rows.append(
                send(
                    sums.at[at],
                    row_in.at[at],
                    row_send.at[at],
                    row_recv.at[at],
                    rows[step - 1],
                )
            )

    for at, (_, sup) in enumerate(pieces):
        for copy in from_core[at]:
            copy.wait_recv()
        held[at, :, :count] = x_ref[sup, owners[at], :, core] + core_x[at]
        held[at, :, count:] = y_ref[sup, owners[at], :, core] + core_y[at]
        from_chips.append(
            [
                send(
                    held.at[at, lax.rem(chip + near + 1, nchip)],
                    chip_in.at[at, near],
                    chip_send.at[at, near],
                    chip_recv.at[at, near],
                    peer,
                )
                for near, peer in enumerate(chips)
            ]
        )
        if at >= 2:
            finish(at - 2)
    finish(len(pieces) - 2)
    finish(len(pieces) - 1)
    for copy in from_rows:
        copy.wait_recv()
    for sup in range(NSUP):
        total = sums[(nrow - 1) * NSUP + sup]
        for step in range(nrow - 1):
            total += row_in[step * NSUP + sup]
        x_out[sup] = total[:count]
        y_out[sup] = total[count:]
    for group in from_core + from_chips + [from_rows]:
        for copy in group:
            copy.wait_send()


def scatter(x, y, nrow, nchip, collective_id):
    count, part = x.shape[-2], y.shape[-2]
    n = nrow * NSUP
    f32 = jnp.float32
    vmem = pl.BlockSpec(memory_space=pltpu.VMEM)
    core, chip, row = (n, 2), (n, nchip - 1), (n - NSUP,)
    return pl.pallas_call(
        functools.partial(scatter_kernel, nrow, nchip),
        out_shape=[
            jax.ShapeDtypeStruct((NSUP, count, W), f32),
            jax.ShapeDtypeStruct((NSUP, part, W), f32),
        ],
        in_specs=[vmem, vmem],
        out_specs=[vmem, vmem],
        scratch_shapes=[
            pltpu.VMEM((n, nchip, count, W), f32),
            pltpu.VMEM((n, nchip, part, W), f32),
            pltpu.VMEM((n, nchip, count + part, W), f32),
            pltpu.VMEM((n, nchip - 1, count + part, W), f32),
            pltpu.VMEM((n, count + part, W), f32),
            pltpu.VMEM((n - NSUP, count + part, W), f32),
            *(pltpu.SemaphoreType.DMA(s) for s in (core, core, chip, chip, row, row)),
        ],
        compiler_params=pltpu.CompilerParams(
            collective_id=collective_id,
            has_side_effects=True,
            vmem_limit_bytes=44 * 1024 * 1024,
        ),
    )(x, y)


def gather_kernel(nrow, nchip, known, x_ref, out_ref, *sems):
    row_send, row_recv, chip_send, chip_recv, core_send, core_recv = sems
    row, _ = place("row")
    chip, _ = place("chip")
    core, _ = place("core")
    rows, chips, cores = others("row", nrow), others("chip", nchip), others("core", 2)
    enter(rows + chips + cores)
    started = []

    def forward(*args):
        started.append(send(*args))
        return started[-1]

    mine = out_ref.at[:, row, chip, core]
    from_rows = [
        forward(x_ref, mine, row_send.at[step], row_recv.at[step], peer)
        for step, peer in enumerate(rows)
    ]
    from_chips = []
    last = []
    for near in range(1 if known else 0, nrow):
        src = x_ref
        slot = mine
        if near > 0:
            from_rows[near - 1].wait_recv()
            slot = out_ref.at[:, lax.rem(row - near + nrow, nrow), chip, core]
            src = slot
        for step, peer in enumerate(chips):
            from_chips.append(
                (
                    near,
                    step + 1,
                    forward(src, slot, chip_send.at[step, near], chip_recv.at[step, near], peer),
                )
            )
        last.append(forward(src, slot, core_send.at[0, near], core_recv.at[0, near], cores[0]))
    for near, step, copy in from_chips:
        copy.wait_recv()
        slot = out_ref.at[
            :, lax.rem(row - near + nrow, nrow), lax.rem(chip - step + nchip, nchip), core
        ]
        last.append(
            forward(slot, slot, core_send.at[step, near], core_recv.at[step, near], cores[0])
        )
    for copy in last:
        copy.wait_recv()
    for copy in started:
        copy.wait_send()


def gather(x, nrow, nchip, collective_id, plane=None):
    shape = (x.shape[0], nrow, nchip, 2) + x.shape[1:]
    row, chip, core = ((nrow - 1,), (nchip - 1, nrow), (nchip, nrow))
    full = pl.pallas_call(
        functools.partial(gather_kernel, nrow, nchip, plane is not None),
        out_shape=jax.ShapeDtypeStruct(shape, x.dtype),
        in_specs=[pl.BlockSpec(memory_space=pl.ANY)],
        out_specs=pl.BlockSpec(memory_space=pl.ANY),
        scratch_shapes=[
            pltpu.SemaphoreType.DMA(n) for n in (row, row, chip, chip, core, core)
        ],
        compiler_params=pltpu.CompilerParams(
            collective_id=collective_id, has_side_effects=True
        ),
    )(x)
    if plane is not None:
        plane = plane.reshape(x.shape[0], 1, nchip, 2, *x.shape[1:])
        return lax.dynamic_update_slice(full, plane, (0, place("row")[0], 0, 0, 0, 0))
    where = (0, place("row")[0], place("chip")[0], place("core")[0], 0, 0)
    return lax.dynamic_update_slice(full, x[:, None, None, None], where)


def dot(a, b, contract):
    def split(x):
        high = x.astype(jnp.bfloat16)
        return high, (x - high.astype(jnp.float32)).astype(jnp.bfloat16)

    def one(x, y):
        return lax.dot_general(
            x, y, ((contract, (0,)), ((), ())), preferred_element_type=jnp.float32
        )

    a_high, a_low = split(a)
    b_high, b_low = split(b)
    return one(a_low, b_high) + one(a_high, b_low) + one(a_high, b_high)


def product_kernel(rows_ref, cols_ref, *refs):
    *tiles, l_ref, p_ref, d_ref = refs
    sup, i = pl.program_id(0), pl.program_id(1)
    row_hit = rows_ref[sup, i] >= 0

    @pl.when(i == 0)
    def _():
        d_ref[...] = jnp.zeros_like(d_ref)

    p_ref[...] = jnp.zeros_like(p_ref)

    @pl.when(row_hit)
    def _():
        for j, a_ref in enumerate(tiles):

            @pl.when(cols_ref[sup, j] >= 0)
            def _():
                p_ref[0] -= dot(a_ref[...], l_ref[0, j * TILE:(j + 1) * TILE, :], (1,))

        block = l_ref[0, pl.ds(pl.multiple_of(i * TILE, TILE), TILE), :]
        d_ref[0] += dot(block, p_ref[0], (0,))


def products(rows, cols, ancestor, lfull):
    def tile(j):
        def index(sup, i, rows_ref, cols_ref):
            row, col = rows_ref[sup, i], cols_ref[sup, j]
            hit = (row >= 0) & (col >= 0)
            return jnp.where(hit, row, 0), jnp.where(hit, col, 0)

        return pl.BlockSpec((TILE, TILE), index)

    total = lfull.shape[1]
    return pl.pallas_call(
        product_kernel,
        out_shape=(
            jax.ShapeDtypeStruct((NSUP, total, W), jnp.float32),
            jax.ShapeDtypeStruct((NSUP, W, W), jnp.float32),
        ),
        grid_spec=pltpu.PrefetchScalarGridSpec(
            num_scalar_prefetch=2,
            grid=(NSUP, NS),
            in_specs=[tile(j) for j in range(NS)]
            + [pl.BlockSpec((1, total, W), lambda sup, i, *_: (sup, 0, 0))],
            out_specs=[
                pl.BlockSpec((1, TILE, W), lambda sup, i, *_: (sup, i, 0)),
                pl.BlockSpec((1, W, W), lambda sup, i, *_: (sup, 0, 0)),
            ],
        ),
        compiler_params=pltpu.CompilerParams(vmem_limit_bytes=40 * 1024 * 1024),
    )(rows, cols, *[ancestor] * NS, lfull)


ROW_TILES = 16
COL_TILES = 8
UNIT = 16
ORDER = (3, 1, 2, 0)


def flip(value, bit):
    return value + bit - 2 * bit * lax.rem(lax.div(value, bit), 2)


def split(x):
    high = x.astype(jnp.bfloat16)
    return high, (x - high.astype(jnp.float32)).astype(jnp.bfloat16)


def dot3(a, b, contract):
    def one(x, y):
        return lax.dot_general(
            x, y, ((contract, (0,)), ((), ())), preferred_element_type=jnp.float32
        )

    (a_high, a_low), (b_high, b_low) = a, b
    return one(a_low, b_high) + one(a_high, b_low) + one(a_high, b_high)


def fused_kernel(rcap, ccap, *refs):
    t_ref, a_ref, l_ref, d_ref, off_ref, diag_ref, a_buf, b_high, b_low, tab, dinv = refs[:11]
    local_sem, send_sem, recv_sem, z_send, z_recv = refs[-5:]
    per_sup = refs[11:-5]
    groups = [per_sup[i * NSUP:(i + 1) * NSUP] for i in range(len(per_sup) // NSUP)]
    l_buf, p_buf, core_in, held, chip_in, mid_buf, total, d_buf, d_core, d_sum, d_in, e_buf, e_in, f_buf = groups
    row = lax.axis_index("prow")
    col = lax.axis_index("pcol")
    core = lax.rem(col, 2)
    chip = lax.div(col, 2)
    rows = [row, flip(row, 1), flip(row, 2), flip(flip(row, 1), 2)]
    chips = [chip, flip(chip, 1), flip(chip, 2), flip(flip(chip, 1), 2)]
    sibling = (row, chip * 2 + 1 - core)

    def on_row(s):
        return rows[s], col

    def on_chip(d):
        return row, chips[d] * 2 + core

    def across(d):
        return row, chips[d] * 2 + 1 - core

    used = {}

    def send(src, dst, peer, group, shared=None):
        at = used.setdefault(shared or len(used), len(used))
        copy = pltpu.make_async_remote_copy(
            src_ref=src,
            dst_ref=dst,
            send_sem=send_sem.at[group],
            recv_sem=recv_sem.at[at],
            device_id=peer,
            device_id_type=MESH,
        )
        copy.start()
        return copy

    def gathered(shared, ref, group=0):
        return pltpu.make_async_remote_copy(
            src_ref=ref,
            dst_ref=ref,
            send_sem=send_sem.at[group],
            recv_sem=recv_sem.at[used[shared]],
            device_id=sibling,
            device_id_type=MESH,
        )

    local = []

    def fetch(src, dst):
        copy = pltpu.make_async_copy(src, dst, local_sem.at[len(local)])
        copy.start()
        local.append(copy)
        return copy

    quarter = l_ref.shape[1]
    half = quarter // 2
    own_l = [
        [
            fetch(l_ref.at[sup, :, :, :, w * 128:(w + 1) * 128],
                  l_buf[sup].at[w, pl.ds(row * quarter, quarter)])
            for w in range(4)
        ]
        for sup in range(NSUP)
    ]
    own_a = [
        fetch(a_ref.at[:, :, j * TILE:(j + 1) * TILE], a_buf.at[j]) for j in range(COL_TILES)
    ]
    d_rows = 256 * core + 64 * row
    lanes = pl.ds(pl.multiple_of(chip * 128, 128), 128)
    own_d = fetch(d_ref.at[:, pl.ds(pl.multiple_of(d_rows, 64), 64), lanes], dinv)

    peers = [on_row(s) for s in (1, 2, 3)] + [on_chip(d) for d in (1, 2, 3)]
    peers += [sibling] + [across(d) for d in (1, 2, 3)]
    enter(peers)

    middle = lax.div(row * (3 - row), 2)
    sources = [
        rows[1],
        rows[2] + middle * (rows[3] - rows[2]),
        rows[3] + middle * (rows[2] - rows[3]),
    ]

    def piece(sup, source, d, begin=0, size=None):
        size = half if size is None else size
        return l_buf[sup].at[chips[d], pl.ds(source * quarter + core * half + begin, size)]

    def z_copy(sup, slot, src, dst, which, s):
        return pltpu.make_async_remote_copy(
            src_ref=src,
            dst_ref=dst,
            send_sem=z_send.at[sup, which],
            recv_sem=z_recv.at[sup, slot],
            device_id=on_row(s),
            device_id_type=MESH,
        )

    def z_own(sup, slot, which, s):
        return z_copy(
            sup, slot, l_ref.at[sup, pl.ds(core * half, half), :, :, lanes],
            piece(sup, row, 0), which, s)

    def z_pass(sup, slot, which):
        block = piece(sup, sources[slot], 0)
        return z_copy(sup, slot, block, block, which, 1)

    def send_rows(sup):
        z_own(sup, 0, 0, 1).start()

        @pl.when(middle == 1)
        def _():
            z_own(sup, 1, 1, 3).start()

        @pl.when(middle == 0)
        def _():
            z_own(sup, 2, 1, 2).start()

    from_x, from_y, from_far = ([[] for _ in range(NSUP)] for _ in range(3))

    def spread_row(sup, slot):
        z_own(sup, slot, 0, 1).wait_recv()
        if slot > 0:
            @pl.when(middle == 1)
            def _():
                z_pass(sup, slot, slot + 1).start()

        block = piece(sup, sources[slot], 0)
        from_x[sup].append(send(block, block, on_chip(1), sup))
        from_y[sup].append(send(block, block, on_chip(2), sup))
        send(block, block, sibling, sup, ("l", sup))

    def spread_chips(sup):
        part = half // 2
        for slot, source in enumerate(sources):
            from_x[sup][slot].wait_recv()
            block = piece(sup, source, 1, 0, part)
            from_far[sup].append((source, 0, send(block, block, on_chip(2), sup)))
            from_y[sup][slot].wait_recv()
            block = piece(sup, source, 2, part, part)
            from_far[sup].append((source, part, send(block, block, on_chip(1), sup)))
            for d in (1, 2):
                block = piece(sup, source, d)
                send(block, block, sibling, sup, ("l", sup))

    def finish_l(sup):
        part = half // 2
        for source, begin, copy in from_far[sup]:
            copy.wait_recv()
            block = piece(sup, source, 3, begin, part)
            send(block, block, sibling, sup, ("l", sup))
        gathered(("l", sup), l_buf[sup].at[:, :3 * half]).wait_recv()
        for copy in own_l[sup]:
            copy.wait()

    def finish_rows(sup):
        z_own(sup, 0, 0, 1).wait_send()
        z_own(sup, 1, 1, 1).wait_send()

        @pl.when(middle == 1)
        def _():
            for slot in (1, 2):
                z_pass(sup, slot, slot + 1).wait_send()

    width = 2 * rcap + 2 * NS + 3 * ccap

    def make_table(sup):
        tiles = [t_ref[sup, k] for k in range(NS)]

        def ranked(base, extent, cap):
            seen = jnp.int32(0)
            found = []
            for k in range(NS):
                at = tiles[k] - base
                hit = ((at >= 0) & (at < extent)).astype(jnp.int32)
                found.append((at, hit, seen))
                seen = seen + hit
            slots = []
            for s in range(cap):
                tile, pos, valid = jnp.int32(0), jnp.int32(0), jnp.int32(0)
                for k, (at, hit, rank) in enumerate(found):
                    here = hit * (rank == s).astype(jnp.int32)
                    tile = tile + here * at
                    pos = pos + here * k
                    valid = valid + here
                slots.append((tile, pos, valid))
            return slots, found

        slots, found = ranked(row * ROW_TILES, ROW_TILES, rcap)
        base = sup * width
        for s, (tile, pos, valid) in enumerate(slots):
            tab[base + s] = tile + (valid - 1) * ROW_TILES
            tab[base + rcap + s] = pos
        base += 2 * rcap
        for k, (_, hit, rank) in enumerate(found):
            tab[base + k] = hit
            tab[base + NS + k] = jnp.minimum(rank, rcap - 1)
        base += 2 * NS
        slots, _ = ranked(col * COL_TILES, COL_TILES, ccap)
        for s, (tile, pos, valid) in enumerate(slots):
            tab[base + s] = tile
            tab[base + ccap + s] = pos
            tab[base + 2 * ccap + s] = valid

    from_core = [[] for _ in range(NSUP)]

    def product(sup):
        base = sup * width
        cols = base + 2 * rcap + 2 * NS
        for t in range(ccap):
            pos = tab[cols + ccap + t]
            for w in range(4):
                block = l_buf[sup][w, pl.ds(pos * UNIT, UNIT)].reshape(TILE, 128)
                high, low = split(block)
                b_high[t * TILE:(t + 1) * TILE, w * 128:(w + 1) * 128] = high
                b_low[t * TILE:(t + 1) * TILE, w * 128:(w + 1) * 128] = low

        @pl.loop(0, rcap)
        def _(s):
            at = tab[base + s]
            tiles = []
            for t in range(ccap):
                hit = (at >= 0) & (tab[cols + 2 * ccap + t] > 0)
                block = a_buf[tab[cols + t], jnp.maximum(at, 0)]
                tiles.append(jnp.where(hit, block, 0.0))
            a = split(jnp.concatenate(tiles, axis=1))
            result = dot3(a, (b_high[...], b_low[...]), (1,))
            for w in range(4):
                block = result[:, w * 128:(w + 1) * 128].reshape(UNIT, 2, 8, 128)
                p_buf[sup][0, w, s] = block[:, 0]
                p_buf[sup][1, w, s] = block[:, 1]

        for d in ORDER:
            from_core[sup].append(
                send(p_buf[sup].at[1 - core, chips[d]], core_in[sup].at[chips[d]], sibling, NSUP + sup)
            )

    from_chips = [[] for _ in range(NSUP)]

    parts = (slice(0, UNIT // 2), slice(UNIT // 2, UNIT))

    def reduce_send(sup):
        for at, d in enumerate(ORDER):
            from_core[sup][at].wait_recv()
            w = chips[d]
            held[sup][w] = p_buf[sup][core, w] + core_in[sup][w]
            for which, near in enumerate((1, 2)):
                if d in (near, 3):
                    src = held[sup].at[w, :, parts[which]]
                    to = chip_in[sup].at[2 * which + (d == 3)]
                    from_chips[sup].append((2 * which + (d == 3), send(src, to, on_chip(near), NSUP + sup)))

    def reduce_pass(sup):
        first = dict(from_chips[sup])
        for which, near in enumerate((1, 2)):
            first[2 * which + 1].wait_recv()
            other = 3 - near
            block = held[sup][chips[other], :, parts[which]]
            mid_buf[sup][which] = block + chip_in[sup][2 * which + 1]
            from_chips[sup].append(
                (
                    4 + which,
                    send(mid_buf[sup].at[which], chip_in[sup].at[4 + which], on_chip(other), NSUP + sup),
                )
            )

    from_d = [None] * NSUP

    def reduce_finish(sup):
        for at, copy in from_chips[sup]:
            if at in (0, 2, 4, 5):
                copy.wait_recv()
        for which in range(2):
            block = held[sup][chip, :, parts[which]] + chip_in[sup][2 * which]
            total[sup][:, parts[which]] = block + chip_in[sup][4 + which]
        base = sup * width
        picked = []
        for s in range(rcap):
            pos = tab[base + rcap + s]
            picked.append(
                jnp.concatenate(
                    [
                        l_buf[sup][w, pl.ds(pos * UNIT, UNIT), core].reshape(128, 128)
                        for w in range(4)
                    ],
                    axis=1,
                )
            )
        left = split(jnp.concatenate(picked, axis=0))
        right = split(total[sup][...].reshape(rcap * 128, 128))
        d_buf[sup][...] = dot3(left, right, (0,)).reshape(2, 256, 128)
        from_d[sup] = send(d_buf[sup].at[1 - core], d_core[sup], sibling, 2 * NSUP)

    def listed(sup, to, put):
        base = sup * width + 2 * rcap
        for j in range(3):
            unit = 3 * to + j
            k = lax.div(unit, 2)
            begin = pl.multiple_of(8 * lax.rem(unit, 2), 8)
            block = total[sup][tab[base + NS + k], pl.ds(begin, 8)]
            put(j, jnp.where(tab[base + k] > 0, block, 0.0))

    def exchange(sup):
        for s in (1, 2, 3):
            def put(j, block):
                e_buf[sup][s - 1, 8 * j:8 * j + 8] = block

            listed(sup, rows[s], put)
            send(e_buf[sup].at[s - 1], e_in[sup].at[s - 1], on_row(s), 2 * NSUP + 1, ("e", sup))

    def diag_rows(sup):
        from_d[sup].wait_recv()
        d_sum[sup][...] = (d_buf[sup][core] + d_core[sup][...]).reshape(4, 64, 128)
        for s in (1, 2, 3):
            send(d_sum[sup].at[rows[s]], d_in[sup].at[s - 1], on_row(s), 2 * NSUP, ("d", sup))

    def diag_piece(sup):
        gathered(("d", sup), d_in[sup]).wait_recv()
        mine = diag_ref.at[sup, pl.ds(pl.multiple_of(d_rows, 64), 64), lanes]
        value = d_sum[sup][row] + d_in[sup][0] + d_in[sup][1] + d_in[sup][2]
        mine[...] = dinv[sup] + value
        for s in (1, 2, 3):
            from_g[sup].append(send(mine, mine, on_row(s), 2 * NSUP))
        for d in (1, 2, 3):
            send(mine, mine, on_chip(d), 2 * NSUP, ("c", sup, d))

    from_g = [[] for _ in range(NSUP)]

    def diag_block(sup, d):
        at = pl.ds(pl.multiple_of(chips[d] * 128, 128), 128)
        return diag_ref.at[sup, pl.ds(pl.multiple_of(256 * core, 256), 256), at]

    def diag_chips(sup):
        for s in (1, 2, 3):
            from_g[sup][s - 1].wait_recv()
            at = pl.ds(pl.multiple_of(256 * core + 64 * rows[s], 64), 64)
            block = diag_ref.at[sup, at, lanes]
            for d in (1, 2, 3):
                send(block, block, on_chip(d), 2 * NSUP, ("c", sup, d))
        block = diag_block(sup, 0)
        send(block, block, sibling, 2 * NSUP, "gs")

    def diag_cores(sup):
        for d in (1, 2, 3):
            block = diag_block(sup, d)
            gathered(("c", sup, d), block).wait_recv()
            send(block, block, sibling, 2 * NSUP, "gs")

    def owners(sup):
        gathered(("e", sup), e_in[sup]).wait_recv()

        def put(j, block):
            at = slice(8 * j, 8 * j + 8)
            rest = e_in[sup][0, at] + e_in[sup][1, at] + e_in[sup][2, at]
            f_buf[sup][at] = -(block + rest)

        listed(sup, row, put)
        place_at = off_ref.at[sup, :, core, :, lanes]

        def share(to):
            return f_buf[sup].at[pl.ds(3 * to, 3)]

        for d in (1, 2, 3):
            for peer in (on_chip(d), across(d)):
                send(share(peer[1]), place_at, peer, 2 * NSUP + 1, "o")
        send(share(sibling[1]), place_at, sibling, 2 * NSUP + 1, "o")
        off_ref[sup, :, core, :, lanes] = f_buf[sup][pl.ds(3 * col, 3)]

    send_rows(0)
    for sup in range(NSUP):
        make_table(sup)
    spread_row(0, 0)
    send_rows(1)
    spread_row(0, 1)
    spread_row(0, 2)
    spread_chips(0)
    for slot in range(3):
        spread_row(1, slot)
    finish_l(0)
    for copy in own_a:
        copy.wait()
    product(0)
    spread_chips(1)
    reduce_send(0)
    finish_l(1)
    product(1)
    reduce_pass(0)
    reduce_send(1)
    reduce_finish(0)
    exchange(0)
    reduce_pass(1)
    diag_rows(0)
    reduce_finish(1)
    diag_rows(1)
    own_d.wait()
    diag_piece(0)
    diag_chips(0)
    owners(0)
    diag_piece(1)
    exchange(1)
    diag_cores(0)
    diag_chips(1)
    owners(1)
    diag_cores(1)
    for sup in range(NSUP):
        finish_rows(sup)
    gathered("gs", l_buf[0].at[:, :32]).wait_recv()
    gathered("o", l_buf[0].at[0, :21]).wait_recv()
    for sup in range(NSUP):
        gathered("o", l_buf[sup].at[:, :63], sup).wait_send()
        gathered("o", p_buf[sup].at[:, :, :, :14], NSUP + sup).wait_send()
    gathered("o", l_buf[0].at[:, :76], 2 * NSUP).wait_send()
    gathered("o", l_buf[0].at[0, :93], 2 * NSUP + 1).wait_send()


def fused(rcap, ccap, tile_lists, ancestor, l_scaled, diag_inv):
    f32 = jnp.float32
    total_rows = l_scaled.shape[1] * 4
    units = total_rows // UNIT
    view = l_scaled.reshape(NSUP, l_scaled.shape[1] // UNIT, 2, 8, W)
    any_space = pl.BlockSpec(memory_space=pl.ANY)
    vmem = pl.BlockSpec(memory_space=pltpu.VMEM)
    block = (rcap, UNIT, 8, 128)
    per_sup = [
        (4, units, 2, 8, 128),
        (2, 4) + block,
        (4,) + block,
        (4,) + block,
        (6, rcap, UNIT // 2, 8, 128),
        (2, rcap, UNIT // 2, 8, 128),
        block,
        (2, 256, 128),
        (256, 128),
        (4, 64, 128),
        (3, 64, 128),
        (3, 24, 8, 128),
        (3, 24, 8, 128),
        (24, 8, 128),
    ]
    scratch = [
        pltpu.VMEM((COL_TILES, ROW_TILES, TILE, TILE), f32),
        pltpu.VMEM((ccap * TILE, W), jnp.bfloat16),
        pltpu.VMEM((ccap * TILE, W), jnp.bfloat16),
        pltpu.SMEM((NSUP * (2 * rcap + 2 * NS + 3 * ccap),), jnp.int32),
        pltpu.VMEM((NSUP, 64, 128), f32),
    ]
    for shape in per_sup:
        scratch += [pltpu.VMEM(shape, f32)] * NSUP
    scratch += [
        pltpu.SemaphoreType.DMA((4 * NSUP + COL_TILES + 1,)),
        pltpu.SemaphoreType.DMA((2 * NSUP + 2,)),
        pltpu.SemaphoreType.DMA((NSUP * (6 + 6 + 1 + 4 + 6 + 1 + 1 + 3 + 3 + 1) + 2,)),
        pltpu.SemaphoreType.DMA((NSUP, 4)),
        pltpu.SemaphoreType.DMA((NSUP, 3)),
    ]
    off, diag = pl.pallas_call(
        functools.partial(fused_kernel, rcap, ccap),
        out_shape=[
            jax.ShapeDtypeStruct((NSUP, 3, 2, 8, W), f32),
            jax.ShapeDtypeStruct((NSUP, W, W), f32),
        ],
        in_specs=[pl.BlockSpec(memory_space=pltpu.SMEM), any_space, any_space, any_space],
        out_specs=[vmem, vmem],
        scratch_shapes=scratch,
        compiler_params=pltpu.CompilerParams(
            collective_id=6 + rcap,
            has_side_effects=True,
            vmem_limit_bytes=60 * 1024 * 1024,
        ),
    )(tile_lists, ancestor.reshape(ROW_TILES, TILE, -1), view, diag_inv)
    return off.reshape(NSUP, 48, W), diag


FOURS = 0x44444444


def packed_counts(tile_lists):
    field = 4 * jnp.arange(NSUP, dtype=jnp.int32)[:, None] + tile_lists // ROW_TILES
    return jnp.sum(jnp.left_shift(jnp.int32(1), 4 * field))


def per_device(nrow, ncol, ancestor_inv, l_scaled, diag_inv, tile_lists):
    if (nrow, ncol) == (4, 8):
        args = (tile_lists, ancestor_inv, l_scaled, diag_inv)
        counts = packed_counts(tile_lists)
        low, middle, top = (functools.partial(fused, cap, cap) for cap in (3, 4, NS - 1))

        def more(*rest):
            fives = counts & jnp.left_shift(counts, 2) & FOURS
            return lax.cond(fives == 0, middle, top, *rest)

        return lax.cond(counts & FOURS == 0, low, more, *args)
    return stepwise(nrow, ncol, ancestor_inv, l_scaled, diag_inv, tile_lists)


def stepwise(nrow, ncol, ancestor_inv, l_scaled, diag_inv, tile_lists):
    nchip = ncol // 2
    tile_rows = ancestor_inv.shape[0] // TILE
    tile_cols = ancestor_inv.shape[1] // TILE
    row_pos = lax.axis_index("prow")
    col_pos = lax.axis_index("pcol")
    count = l_scaled.shape[1] // ncol
    part = W // (nrow * ncol)
    total = l_scaled.shape[1] * nrow

    share = lax.dynamic_slice_in_dim(l_scaled, col_pos * count, count, 1)
    lfull = gather(share, nrow, nchip, 1, l_scaled).reshape(NSUP, total, W)

    rows = tile_lists - row_pos * tile_rows
    rows = jnp.where((rows >= 0) & (rows < tile_rows), rows, -1)
    cols = tile_lists - col_pos * tile_cols
    cols = jnp.where((cols >= 0) & (cols < tile_cols), cols, -1)
    rows = jnp.where(jnp.max(cols, axis=1, keepdims=True) >= 0, rows, -1)
    partial, terms = products(rows, cols, ancestor_inv, lfull)

    mine, term = scatter(
        partial.reshape(NSUP, nrow, nchip, 2, count, W),
        terms.reshape(NSUP, nrow, nchip, 2, part, W),
        nrow,
        nchip,
        2,
    )
    diag = gather(term, nrow, nchip, 5).reshape(NSUP, W, W)
    return mine, diag_inv - diag


def solution(mesh):
    placed = (P("prow", "pcol"), P(None, "prow", None), P(), P())
    return jax.shard_map(
        functools.partial(per_device, mesh.shape["prow"], mesh.shape["pcol"]),
        mesh=mesh,
        in_specs=placed,
        out_specs=(P(None, ("prow", "pcol"), None), P()),
        check_vma=False,
    )
```

```python
import functools

import jax
import jax.numpy as jnp
from jax import lax
from jax.experimental import pallas as pl
from jax.experimental.pallas import tpu as pltpu
from jax.sharding import PartitionSpec as P

TILE = 256
W = 512
NS = 6
NSUP = 2
MESH = pl.DeviceIdType.MESH


def place(stage):
    row = lax.axis_index("prow")
    col = lax.axis_index("pcol")
    core = lax.rem(col, 2)
    chip = col // 2
    if stage == "row":
        return row, lambda m: (m, col)
    if stage == "chip":
        return chip, lambda m: (row, m * 2 + core)
    return core, lambda m: (row, chip * 2 + m)


def enter(peers):
    barrier = pltpu.get_barrier_semaphore()
    for peer in peers:
        pl.semaphore_signal(barrier, inc=1, device_id=peer, device_id_type=MESH)
    pl.semaphore_wait(barrier, len(peers))


def others(stage, size):
    me, device = place(stage)
    return [device(lax.rem(me + step, size)) for step in range(1, size)]


def send(src, dst, send_sem, recv_sem, peer):
    copy = pltpu.make_async_remote_copy(
        src_ref=src,
        dst_ref=dst,
        send_sem=send_sem,
        recv_sem=recv_sem,
        device_id=peer,
        device_id_type=MESH,
    )
    copy.start()
    return copy


def scatter_kernel(
    nrow, nchip, x_ref, y_ref, x_out, y_out, core_x, core_y, held, chip_in, sums, row_in, *sems
):
    core_send, core_recv, chip_send, chip_recv, row_send, row_recv = sems
    row, _ = place("row")
    chip, _ = place("chip")
    core, _ = place("core")
    rows, chips, cores = others("row", nrow), others("chip", nchip), others("core", 2)
    enter(rows + chips + cores)
    count = x_ref.shape[-2]
    pieces = [(step, sup) for step in [*range(1, nrow), 0] for sup in range(NSUP)]
    owners = [lax.rem(row + step, nrow) for step, _ in pieces]
    from_core = []
    for at, (_, sup) in enumerate(pieces):
        to = owners[at]
        from_core.append(
            [
                send(
                    src.at[sup, to, :, 1 - core],
                    dst.at[at],
                    core_send.at[at, which],
                    core_recv.at[at, which],
                    cores[0],
                )
                for which, (src, dst) in enumerate(((x_ref, core_x), (y_ref, core_y)))
            ]
        )
    from_chips = []
    from_rows = []

    def finish(at):
        step, sup = pieces[at]
        for copy in from_chips[at]:
            copy.wait_recv()
        total = held[at, chip]
        for near in range(nchip - 1):
            total += chip_in[at, near]
        sums[at] = total
        if step > 0:
            from_rows.append(
                send(
                    sums.at[at],
                    row_in.at[at],
                    row_send.at[at],
                    row_recv.at[at],
                    rows[step - 1],
                )
            )

    for at, (_, sup) in enumerate(pieces):
        for copy in from_core[at]:
            copy.wait_recv()
        held[at, :, :count] = x_ref[sup, owners[at], :, core] + core_x[at]
        held[at, :, count:] = y_ref[sup, owners[at], :, core] + core_y[at]
        from_chips.append(
            [
                send(
                    held.at[at, lax.rem(chip + near + 1, nchip)],
                    chip_in.at[at, near],
                    chip_send.at[at, near],
                    chip_recv.at[at, near],
                    peer,
                )
                for near, peer in enumerate(chips)
            ]
        )
        if at >= 2:
            finish(at - 2)
    finish(len(pieces) - 2)
    finish(len(pieces) - 1)
    for copy in from_rows:
        copy.wait_recv()
    for sup in range(NSUP):
        total = sums[(nrow - 1) * NSUP + sup]
        for step in range(nrow - 1):
            total += row_in[step * NSUP + sup]
        x_out[sup] = total[:count]
        y_out[sup] = total[count:]
    for group in from_core + from_chips + [from_rows]:
        for copy in group:
            copy.wait_send()


def scatter(x, y, nrow, nchip, collective_id):
    count, part = x.shape[-2], y.shape[-2]
    n = nrow * NSUP
    f32 = jnp.float32
    vmem = pl.BlockSpec(memory_space=pltpu.VMEM)
    core, chip, row = (n, 2), (n, nchip - 1), (n - NSUP,)
    return pl.pallas_call(
        functools.partial(scatter_kernel, nrow, nchip),
        out_shape=[
            jax.ShapeDtypeStruct((NSUP, count, W), f32),
            jax.ShapeDtypeStruct((NSUP, part, W), f32),
        ],
        in_specs=[vmem, vmem],
        out_specs=[vmem, vmem],
        scratch_shapes=[
            pltpu.VMEM((n, nchip, count, W), f32),
            pltpu.VMEM((n, nchip, part, W), f32),
            pltpu.VMEM((n, nchip, count + part, W), f32),
            pltpu.VMEM((n, nchip - 1, count + part, W), f32),
            pltpu.VMEM((n, count + part, W), f32),
            pltpu.VMEM((n - NSUP, count + part, W), f32),
            *(pltpu.SemaphoreType.DMA(s) for s in (core, core, chip, chip, row, row)),
        ],
        compiler_params=pltpu.CompilerParams(
            collective_id=collective_id,
            has_side_effects=True,
            vmem_limit_bytes=44 * 1024 * 1024,
        ),
    )(x, y)


def gather_kernel(nrow, nchip, known, x_ref, out_ref, *sems):
    row_send, row_recv, chip_send, chip_recv, core_send, core_recv = sems
    row, _ = place("row")
    chip, _ = place("chip")
    core, _ = place("core")
    rows, chips, cores = others("row", nrow), others("chip", nchip), others("core", 2)
    enter(rows + chips + cores)
    started = []

    def forward(*args):
        started.append(send(*args))
        return started[-1]

    mine = out_ref.at[:, row, chip, core]
    from_rows = [
        forward(x_ref, mine, row_send.at[step], row_recv.at[step], peer)
        for step, peer in enumerate(rows)
    ]
    from_chips = []
    last = []
    for near in range(1 if known else 0, nrow):
        src = x_ref
        slot = mine
        if near > 0:
            from_rows[near - 1].wait_recv()
            slot = out_ref.at[:, lax.rem(row - near + nrow, nrow), chip, core]
            src = slot
        for step, peer in enumerate(chips):
            from_chips.append(
                (
                    near,
                    step + 1,
                    forward(src, slot, chip_send.at[step, near], chip_recv.at[step, near], peer),
                )
            )
        last.append(forward(src, slot, core_send.at[0, near], core_recv.at[0, near], cores[0]))
    for near, step, copy in from_chips:
        copy.wait_recv()
        slot = out_ref.at[
            :, lax.rem(row - near + nrow, nrow), lax.rem(chip - step + nchip, nchip), core
        ]
        last.append(
            forward(slot, slot, core_send.at[step, near], core_recv.at[step, near], cores[0])
        )
    for copy in last:
        copy.wait_recv()
    for copy in started:
        copy.wait_send()


def gather(x, nrow, nchip, collective_id, plane=None):
    shape = (x.shape[0], nrow, nchip, 2) + x.shape[1:]
    row, chip, core = ((nrow - 1,), (nchip - 1, nrow), (nchip, nrow))
    full = pl.pallas_call(
        functools.partial(gather_kernel, nrow, nchip, plane is not None),
        out_shape=jax.ShapeDtypeStruct(shape, x.dtype),
        in_specs=[pl.BlockSpec(memory_space=pl.ANY)],
        out_specs=pl.BlockSpec(memory_space=pl.ANY),
        scratch_shapes=[
            pltpu.SemaphoreType.DMA(n) for n in (row, row, chip, chip, core, core)
        ],
        compiler_params=pltpu.CompilerParams(
            collective_id=collective_id, has_side_effects=True
        ),
    )(x)
    if plane is not None:
        plane = plane.reshape(x.shape[0], 1, nchip, 2, *x.shape[1:])
        return lax.dynamic_update_slice(full, plane, (0, place("row")[0], 0, 0, 0, 0))
    where = (0, place("row")[0], place("chip")[0], place("core")[0], 0, 0)
    return lax.dynamic_update_slice(full, x[:, None, None, None], where)


def dot(a, b, contract):
    def split(x):
        high = x.astype(jnp.bfloat16)
        return high, (x - high.astype(jnp.float32)).astype(jnp.bfloat16)

    def one(x, y):
        return lax.dot_general(
            x, y, ((contract, (0,)), ((), ())), preferred_element_type=jnp.float32
        )

    a_high, a_low = split(a)
    b_high, b_low = split(b)
    return one(a_low, b_high) + one(a_high, b_low) + one(a_high, b_high)


def product_kernel(rows_ref, cols_ref, *refs):
    *tiles, l_ref, p_ref, d_ref = refs
    sup, i = pl.program_id(0), pl.program_id(1)
    row_hit = rows_ref[sup, i] >= 0

    @pl.when(i == 0)
    def _():
        d_ref[...] = jnp.zeros_like(d_ref)

    p_ref[...] = jnp.zeros_like(p_ref)

    @pl.when(row_hit)
    def _():
        for j, a_ref in enumerate(tiles):

            @pl.when(cols_ref[sup, j] >= 0)
            def _():
                p_ref[0] -= dot(a_ref[...], l_ref[0, j * TILE:(j + 1) * TILE, :], (1,))

        block = l_ref[0, pl.ds(pl.multiple_of(i * TILE, TILE), TILE), :]
        d_ref[0] += dot(block, p_ref[0], (0,))


def products(rows, cols, ancestor, lfull):
    def tile(j):
        def index(sup, i, rows_ref, cols_ref):
            row, col = rows_ref[sup, i], cols_ref[sup, j]
            hit = (row >= 0) & (col >= 0)
            return jnp.where(hit, row, 0), jnp.where(hit, col, 0)

        return pl.BlockSpec((TILE, TILE), index)

    total = lfull.shape[1]
    return pl.pallas_call(
        product_kernel,
        out_shape=(
            jax.ShapeDtypeStruct((NSUP, total, W), jnp.float32),
            jax.ShapeDtypeStruct((NSUP, W, W), jnp.float32),
        ),
        grid_spec=pltpu.PrefetchScalarGridSpec(
            num_scalar_prefetch=2,
            grid=(NSUP, NS),
            in_specs=[tile(j) for j in range(NS)]
            + [pl.BlockSpec((1, total, W), lambda sup, i, *_: (sup, 0, 0))],
            out_specs=[
                pl.BlockSpec((1, TILE, W), lambda sup, i, *_: (sup, i, 0)),
                pl.BlockSpec((1, W, W), lambda sup, i, *_: (sup, 0, 0)),
            ],
        ),
        compiler_params=pltpu.CompilerParams(vmem_limit_bytes=40 * 1024 * 1024),
    )(rows, cols, *[ancestor] * NS, lfull)


ROW_TILES = 16
COL_TILES = 8
UNIT = 16
ORDER = (3, 1, 2, 0)
FAR = (1,)


def flip(value, bit):
    return value + bit - 2 * bit * lax.rem(lax.div(value, bit), 2)


def split(x):
    high = x.astype(jnp.bfloat16)
    return high, (x - high.astype(jnp.float32)).astype(jnp.bfloat16)


def dot3(a, b, contract):
    def one(x, y):
        return lax.dot_general(
            x, y, ((contract, (0,)), ((), ())), preferred_element_type=jnp.float32
        )

    (a_high, a_low), (b_high, b_low) = a, b
    return one(a_low, b_high) + one(a_high, b_low) + one(a_high, b_high)


def fused_kernel(rcap, ccap, *refs):
    t_ref, a_ref, l_ref, d_ref, off_ref, diag_ref, a_buf, b_high, b_low, tab, dinv = refs[:11]
    local_sem, send_sem, recv_sem, z_send, z_recv = refs[-5:]
    per_sup = refs[11:-5]
    groups = [per_sup[i * NSUP:(i + 1) * NSUP] for i in range(len(per_sup) // NSUP)]
    l_buf, p_buf, core_in, held, chip_in, mid_buf, total, d_buf, d_core, d_sum, d_in, e_buf, e_in, f_buf = groups
    row = lax.axis_index("prow")
    col = lax.axis_index("pcol")
    core = lax.rem(col, 2)
    chip = lax.div(col, 2)
    rows = [row, flip(row, 1), flip(row, 2), flip(flip(row, 1), 2)]
    chips = [chip, flip(chip, 1), flip(chip, 2), flip(flip(chip, 1), 2)]
    sibling = (row, chip * 2 + 1 - core)

    def on_row(s):
        return rows[s], col

    def on_chip(d):
        return row, chips[d] * 2 + core

    def across(d):
        return row, chips[d] * 2 + 1 - core

    used = {}

    def send(src, dst, peer, group, shared=None):
        at = used.setdefault(shared or len(used), len(used))
        copy = pltpu.make_async_remote_copy(
            src_ref=src,
            dst_ref=dst,
            send_sem=send_sem.at[group],
            recv_sem=recv_sem.at[at],
            device_id=peer,
            device_id_type=MESH,
        )
        copy.start()
        return copy

    def gathered(shared, ref, group=0):
        return pltpu.make_async_remote_copy(
            src_ref=ref,
            dst_ref=ref,
            send_sem=send_sem.at[group],
            recv_sem=recv_sem.at[used[shared]],
            device_id=sibling,
            device_id_type=MESH,
        )

    local = []

    def fetch(src, dst):
        copy = pltpu.make_async_copy(src, dst, local_sem.at[len(local)])
        copy.start()
        local.append(copy)
        return copy

    quarter = l_ref.shape[1]
    half = quarter // 2
    own_l = [
        [
            fetch(l_ref.at[sup, :, :, :, w * 128:(w + 1) * 128],
                  l_buf[sup].at[w, pl.ds(row * quarter, quarter)])
            for w in range(4)
        ]
        for sup in range(NSUP)
    ]
    own_a = [
        fetch(a_ref.at[:, :, j * TILE:(j + 1) * TILE], a_buf.at[j]) for j in range(COL_TILES)
    ]
    d_rows = 256 * core + 64 * row
    lanes = pl.ds(pl.multiple_of(chip * 128, 128), 128)
    own_d = fetch(d_ref.at[:, pl.ds(pl.multiple_of(d_rows, 64), 64), lanes], dinv)

    peers = [on_row(s) for s in (1, 2, 3)] + [on_chip(d) for d in (1, 2, 3)]
    peers += [sibling] + [across(d) for d in (1, 2, 3)]
    enter(peers)

    middle = lax.div(row * (3 - row), 2)
    sources = [
        rows[1],
        rows[2] + middle * (rows[3] - rows[2]),
        rows[3] + middle * (rows[2] - rows[3]),
    ]

    def piece(sup, source, d, begin=0, size=None):
        size = half if size is None else size
        return l_buf[sup].at[chips[d], pl.ds(source * quarter + core * half + begin, size)]

    routes = [(sup, 0) for sup in range(NSUP)] + [(sup, 3) for sup in FAR]

    def z_copy(route, slot, src, dst, which, s):
        return pltpu.make_async_remote_copy(
            src_ref=src,
            dst_ref=dst,
            send_sem=z_send.at[route, which],
            recv_sem=z_recv.at[route, slot],
            device_id=on_row(s),
            device_id_type=MESH,
        )

    def z_own(route, slot, which, s):
        sup, d = routes[route]
        at = pl.ds(pl.multiple_of(chips[d] * 128, 128), 128)
        return z_copy(
            route, slot, l_ref.at[sup, pl.ds(core * half, half), :, :, at],
            piece(sup, row, d), which, s)

    def z_pass(route, slot, which):
        sup, d = routes[route]
        block = piece(sup, sources[slot], d)
        return z_copy(route, slot, block, block, which, 1)

    def send_rows(route):
        z_own(route, 0, 0, 1).start()

        @pl.when(middle == 1)
        def _():
            z_own(route, 1, 1, 3).start()

        @pl.when(middle == 0)
        def _():
            z_own(route, 2, 1, 2).start()

    from_x, from_y, from_far = ([[] for _ in range(NSUP)] for _ in range(3))

    def pass_row(route, slot):
        @pl.when(middle == 1)
        def _():
            z_own(route, slot, 0, 1).wait_recv()
            z_pass(route, slot, slot + 1).start()

    def arrive(route, slot):
        if slot > 0:
            @pl.when(middle == 0)
            def _():
                z_own(route, slot, 0, 1).wait_recv()
        else:
            z_own(route, slot, 0, 1).wait_recv()

    def spread_row(sup, slot):
        arrive(sup, slot)
        block = piece(sup, sources[slot], 0)
        from_x[sup].append(send(block, block, on_chip(1), sup))
        from_y[sup].append(send(block, block, on_chip(2), sup))
        send(block, block, sibling, sup, ("l", sup))

    def spread_chips(sup, slots=(0, 1, 2)):
        part = half // 2
        for slot in slots:
            source = sources[slot]
            from_x[sup][slot].wait_recv()
            if sup not in FAR:
                block = piece(sup, source, 1, 0, part)
                from_far[sup].append((source, 0, send(block, block, on_chip(2), sup)))
            from_y[sup][slot].wait_recv()
            if sup not in FAR:
                block = piece(sup, source, 2, part, part)
                from_far[sup].append((source, part, send(block, block, on_chip(1), sup)))
            for d in (1, 2):
                block = piece(sup, source, d)
                send(block, block, sibling, sup, ("l", sup))

    def finish_l(sup):
        part = half // 2
        if sup in FAR:
            route = NSUP + FAR.index(sup)
            for slot in range(3):
                arrive(route, slot)
                block = piece(sup, sources[slot], 3)
                send(block, block, sibling, sup, ("l", sup))
        for source, begin, copy in from_far[sup]:
            copy.wait_recv()
            block = piece(sup, source, 3, begin, part)
            send(block, block, sibling, sup, ("l", sup))
        gathered(("l", sup), l_buf[sup].at[:, :3 * half]).wait_recv()
        for copy in own_l[sup]:
            copy.wait()

    def finish_rows(route):
        z_own(route, 0, 0, 1).wait_send()
        z_own(route, 1, 1, 1).wait_send()

        @pl.when(middle == 1)
        def _():
            for slot in (1, 2):
                z_pass(route, slot, slot + 1).wait_send()

    width = 2 * rcap + 2 * NS + 3 * ccap

    def make_table(sup):
        tiles = [t_ref[sup, k] for k in range(NS)]

        def ranked(base, extent, cap):
            seen = jnp.int32(0)
            found = []
            for k in range(NS):
                at = tiles[k] - base
                hit = ((at >= 0) & (at < extent)).astype(jnp.int32)
                found.append((at, hit, seen))
                seen = seen + hit
            slots = []
            for s in range(cap):
                tile, pos, valid = jnp.int32(0), jnp.int32(0), jnp.int32(0)
                for k, (at, hit, rank) in enumerate(found):
                    here = hit * (rank == s).astype(jnp.int32)
                    tile = tile + here * at
                    pos = pos + here * k
                    valid = valid + here
                slots.append((tile, pos, valid))
            return slots, found

        slots, found = ranked(row * ROW_TILES, ROW_TILES, rcap)
        base = sup * width
        for s, (tile, pos, valid) in enumerate(slots):
            tab[base + s] = tile + (valid - 1) * ROW_TILES
            tab[base + rcap + s] = pos
        base += 2 * rcap
        for k, (_, hit, rank) in enumerate(found):
            tab[base + k] = hit
            tab[base + NS + k] = jnp.minimum(rank, rcap - 1)
        base += 2 * NS
        slots, _ = ranked(col * COL_TILES, COL_TILES, ccap)
        for s, (tile, pos, valid) in enumerate(slots):
            tab[base + s] = tile
            tab[base + ccap + s] = pos
            tab[base + 2 * ccap + s] = valid

    from_core = [[] for _ in range(NSUP)]

    def product(sup):
        base = sup * width
        cols = base + 2 * rcap + 2 * NS
        for t in range(ccap):
            pos = tab[cols + ccap + t]
            for w in range(4):
                block = l_buf[sup][w, pl.ds(pos * UNIT, UNIT)].reshape(TILE, 128)
                high, low = split(block)
                b_high[t * TILE:(t + 1) * TILE, w * 128:(w + 1) * 128] = high
                b_low[t * TILE:(t + 1) * TILE, w * 128:(w + 1) * 128] = low

        for s in range(rcap):
            at = tab[base + s]
            tiles = []
            for t in range(ccap):
                hit = (at >= 0) & (tab[cols + 2 * ccap + t] > 0)
                block = a_buf[tab[cols + t], jnp.maximum(at, 0)]
                tiles.append(jnp.where(hit, block, 0.0))
            a = split(jnp.concatenate(tiles, axis=1))
            result = dot3(a, (b_high[...], b_low[...]), (1,))
            for w in range(4):
                block = result[:, w * 128:(w + 1) * 128].reshape(UNIT, 2, 8, 128)
                p_buf[sup][0, w, s] = block[:, 0]
                p_buf[sup][1, w, s] = block[:, 1]

            src = p_buf[sup].at[1 - core, :, s]
            from_core[sup].append(send(src, core_in[sup].at[:, s], sibling, NSUP + sup))

    from_chips = [[] for _ in range(NSUP)]

    parts = (slice(0, UNIT // 2), slice(UNIT // 2, UNIT))

    def reduce_send(sup):
        for s in range(rcap):
            from_core[sup][s].wait_recv()
            held[sup][:, s] = p_buf[sup][core, :, s] + core_in[sup][:, s]
        for d in ORDER[:3]:
            w = chips[d]
            for which, near in enumerate((1, 2)):
                if d in (near, 3):
                    src = held[sup].at[w, :, parts[which]]
                    to = chip_in[sup].at[2 * which + (d == 3)]
                    from_chips[sup].append((2 * which + (d == 3), send(src, to, on_chip(near), NSUP + sup)))

    def reduce_pass(sup):
        first = dict(from_chips[sup])
        for which, near in enumerate((1, 2)):
            first[2 * which + 1].wait_recv()
            other = 3 - near
            block = held[sup][chips[other], :, parts[which]]
            mid_buf[sup][which] = block + chip_in[sup][2 * which + 1]
            from_chips[sup].append(
                (
                    4 + which,
                    send(mid_buf[sup].at[which], chip_in[sup].at[4 + which], on_chip(other), NSUP + sup),
                )
            )

    from_d = [None] * NSUP

    def reduce_finish(sup):
        for at, copy in from_chips[sup]:
            if at in (0, 2, 4, 5):
                copy.wait_recv()
        for which in range(2):
            block = held[sup][chip, :, parts[which]] + chip_in[sup][2 * which]
            total[sup][:, parts[which]] = block + chip_in[sup][4 + which]
        base = sup * width
        picked = []
        for s in range(rcap):
            pos = tab[base + rcap + s]
            picked.append(
                jnp.concatenate(
                    [
                        l_buf[sup][w, pl.ds(pos * UNIT, UNIT), core].reshape(128, 128)
                        for w in range(4)
                    ],
                    axis=1,
                )
            )
        left = split(jnp.concatenate(picked, axis=0))
        right = split(total[sup][...].reshape(rcap * 128, 128))
        d_buf[sup][...] = dot3(left, right, (0,)).reshape(2, 256, 128)
        from_d[sup] = send(d_buf[sup].at[1 - core], d_core[sup], sibling, 2 * NSUP)

    def listed(sup, to, put):
        base = sup * width + 2 * rcap
        for j in range(3):
            unit = 3 * to + j
            k = lax.div(unit, 2)
            begin = pl.multiple_of(8 * lax.rem(unit, 2), 8)
            block = total[sup][tab[base + NS + k], pl.ds(begin, 8)]
            put(j, jnp.where(tab[base + k] > 0, block, 0.0))

    def exchange(sup):
        for s in (1, 2, 3):
            def put(j, block):
                e_buf[sup][s - 1, 8 * j:8 * j + 8] = block

            listed(sup, rows[s], put)
            send(e_buf[sup].at[s - 1], e_in[sup].at[s - 1], on_row(s), 2 * NSUP + 1, ("e", sup))

    def diag_rows(sup):
        from_d[sup].wait_recv()
        d_sum[sup][...] = (d_buf[sup][core] + d_core[sup][...]).reshape(4, 64, 128)
        for s in (1, 2, 3):
            send(d_sum[sup].at[rows[s]], d_in[sup].at[s - 1], on_row(s), 2 * NSUP, ("d", sup))

    def diag_piece(sup):
        gathered(("d", sup), d_in[sup]).wait_recv()
        mine = diag_ref.at[sup, pl.ds(pl.multiple_of(d_rows, 64), 64), lanes]
        value = d_sum[sup][row] + d_in[sup][0] + d_in[sup][1] + d_in[sup][2]
        mine[...] = dinv[sup] + value
        for s in (1, 2, 3):
            from_g[sup].append(send(mine, mine, on_row(s), 2 * NSUP))
        for d in (1, 2, 3):
            send(mine, mine, on_chip(d), 2 * NSUP, ("c", sup, d))

    from_g = [[] for _ in range(NSUP)]

    def diag_block(sup, d):
        at = pl.ds(pl.multiple_of(chips[d] * 128, 128), 128)
        return diag_ref.at[sup, pl.ds(pl.multiple_of(256 * core, 256), 256), at]

    def diag_chips(sup):
        for s in (1, 2, 3):
            from_g[sup][s - 1].wait_recv()
            at = pl.ds(pl.multiple_of(256 * core + 64 * rows[s], 64), 64)
            block = diag_ref.at[sup, at, lanes]
            for d in (1, 2, 3):
                send(block, block, on_chip(d), 2 * NSUP, ("c", sup, d))
        block = diag_block(sup, 0)
        send(block, block, sibling, 2 * NSUP, "gs")

    def diag_cores(sup):
        for d in (1, 2, 3):
            block = diag_block(sup, d)
            gathered(("c", sup, d), block).wait_recv()
            send(block, block, sibling, 2 * NSUP, "gs")

    def owners(sup):
        gathered(("e", sup), e_in[sup]).wait_recv()

        def put(j, block):
            at = slice(8 * j, 8 * j + 8)
            rest = e_in[sup][0, at] + e_in[sup][1, at] + e_in[sup][2, at]
            f_buf[sup][at] = -(block + rest)

        listed(sup, row, put)
        place_at = off_ref.at[sup, :, core, :, lanes]

        def share(to):
            return f_buf[sup].at[pl.ds(3 * to, 3)]

        for d in (1, 2, 3):
            for peer in (on_chip(d), across(d)):
                send(share(peer[1]), place_at, peer, 2 * NSUP + 1, "o")
        send(share(sibling[1]), place_at, sibling, 2 * NSUP + 1, "o")
        off_ref[sup, :, core, :, lanes] = f_buf[sup][pl.ds(3 * col, 3)]

    send_rows(0)
    for sup in range(NSUP):
        make_table(sup)
    spread_row(0, 0)
    send_rows(1)
    pass_row(0, 1)
    spread_row(0, 1)
    pass_row(0, 2)
    spread_row(0, 2)
    send_rows(2)
    spread_chips(0)
    pass_row(1, 1)
    pass_row(1, 2)
    for slot in range(3):
        spread_row(1, slot)
    pass_row(2, 1)
    pass_row(2, 2)
    finish_l(0)
    for copy in own_a:
        copy.wait()
    product(0)
    spread_chips(1)
    reduce_send(0)
    finish_l(1)
    product(1)
    reduce_pass(0)
    reduce_send(1)
    reduce_finish(0)
    exchange(0)
    reduce_pass(1)
    diag_rows(0)
    reduce_finish(1)
    diag_rows(1)
    own_d.wait()
    diag_piece(0)
    diag_chips(0)
    owners(0)
    diag_piece(1)
    exchange(1)
    diag_cores(0)
    diag_chips(1)
    owners(1)
    diag_cores(1)
    for route in range(len(routes)):
        finish_rows(route)
    gathered("gs", l_buf[0].at[:, :32]).wait_recv()
    gathered("o", l_buf[0].at[0, :21]).wait_recv()
    for sup in range(NSUP):
        gathered("o", l_buf[sup].at[:, :54 if sup in FAR else 63], sup).wait_send()
        gathered("o", p_buf[sup].at[:, :, :, :14], NSUP + sup).wait_send()
    gathered("o", l_buf[0].at[:, :76], 2 * NSUP).wait_send()
    gathered("o", l_buf[0].at[0, :93], 2 * NSUP + 1).wait_send()


def fused(rcap, ccap, tile_lists, ancestor, l_scaled, diag_inv):
    f32 = jnp.float32
    total_rows = l_scaled.shape[1] * 4
    units = total_rows // UNIT
    view = l_scaled.reshape(NSUP, l_scaled.shape[1] // UNIT, 2, 8, W)
    any_space = pl.BlockSpec(memory_space=pl.ANY)
    vmem = pl.BlockSpec(memory_space=pltpu.VMEM)
    block = (rcap, UNIT, 8, 128)
    per_sup = [
        (4, units, 2, 8, 128),
        (2, 4) + block,
        (4,) + block,
        (4,) + block,
        (6, rcap, UNIT // 2, 8, 128),
        (2, rcap, UNIT // 2, 8, 128),
        block,
        (2, 256, 128),
        (256, 128),
        (4, 64, 128),
        (3, 64, 128),
        (3, 24, 8, 128),
        (3, 24, 8, 128),
        (24, 8, 128),
    ]
    scratch = [
        pltpu.VMEM((COL_TILES, ROW_TILES, TILE, TILE), f32),
        pltpu.VMEM((ccap * TILE, W), jnp.bfloat16),
        pltpu.VMEM((ccap * TILE, W), jnp.bfloat16),
        pltpu.SMEM((NSUP * (2 * rcap + 2 * NS + 3 * ccap),), jnp.int32),
        pltpu.VMEM((NSUP, 64, 128), f32),
    ]
    for shape in per_sup:
        scratch += [pltpu.VMEM(shape, f32)] * NSUP
    scratch += [
        pltpu.SemaphoreType.DMA((4 * NSUP + COL_TILES + 1,)),
        pltpu.SemaphoreType.DMA((2 * NSUP + 2,)),
        pltpu.SemaphoreType.DMA((NSUP * (6 + 1 + rcap + 6 + 1 + 1 + 3 + 3 + 1) + 6 * (NSUP - len(FAR)) + 2,)),
        pltpu.SemaphoreType.DMA((NSUP + len(FAR), 4)),
        pltpu.SemaphoreType.DMA((NSUP + len(FAR), 3)),
    ]
    off, diag = pl.pallas_call(
        functools.partial(fused_kernel, rcap, ccap),
        out_shape=[
            jax.ShapeDtypeStruct((NSUP, 3, 2, 8, W), f32),
            jax.ShapeDtypeStruct((NSUP, W, W), f32),
        ],
        in_specs=[pl.BlockSpec(memory_space=pltpu.SMEM), any_space, any_space, any_space],
        out_specs=[vmem, vmem],
        scratch_shapes=scratch,
        compiler_params=pltpu.CompilerParams(
            collective_id=6 + rcap,
            has_side_effects=True,
            vmem_limit_bytes=60 * 1024 * 1024,
        ),
    )(tile_lists, ancestor.reshape(ROW_TILES, TILE, -1), view, diag_inv)
    return off.reshape(NSUP, 48, W), diag


FOURS = 0x44444444


def packed_counts(tile_lists):
    field = 4 * jnp.arange(NSUP, dtype=jnp.int32)[:, None] + tile_lists // ROW_TILES
    return jnp.sum(jnp.left_shift(jnp.int32(1), 4 * field))


def per_device(nrow, ncol, ancestor_inv, l_scaled, diag_inv, tile_lists):
    if (nrow, ncol) == (4, 8):
        args = (tile_lists, ancestor_inv, l_scaled, diag_inv)
        counts = packed_counts(tile_lists)
        low, middle, top = (functools.partial(fused, cap, cap) for cap in (3, 4, NS - 1))

        def more(*rest):
            fives = counts & jnp.left_shift(counts, 2) & FOURS
            return lax.cond(fives == 0, middle, top, *rest)

        return lax.cond(counts & FOURS == 0, low, more, *args)
    return stepwise(nrow, ncol, ancestor_inv, l_scaled, diag_inv, tile_lists)


def stepwise(nrow, ncol, ancestor_inv, l_scaled, diag_inv, tile_lists):
    nchip = ncol // 2
    tile_rows = ancestor_inv.shape[0] // TILE
    tile_cols = ancestor_inv.shape[1] // TILE
    row_pos = lax.axis_index("prow")
    col_pos = lax.axis_index("pcol")
    count = l_scaled.shape[1] // ncol
    part = W // (nrow * ncol)
    total = l_scaled.shape[1] * nrow

    share = lax.dynamic_slice_in_dim(l_scaled, col_pos * count, count, 1)
    lfull = gather(share, nrow, nchip, 1, l_scaled).reshape(NSUP, total, W)

    rows = tile_lists - row_pos * tile_rows
    rows = jnp.where((rows >= 0) & (rows < tile_rows), rows, -1)
    cols = tile_lists - col_pos * tile_cols
    cols = jnp.where((cols >= 0) & (cols < tile_cols), cols, -1)
    rows = jnp.where(jnp.max(cols, axis=1, keepdims=True) >= 0, rows, -1)
    partial, terms = products(rows, cols, ancestor_inv, lfull)

    mine, term = scatter(
        partial.reshape(NSUP, nrow, nchip, 2, count, W),
        terms.reshape(NSUP, nrow, nchip, 2, part, W),
        nrow,
        nchip,
        2,
    )
    diag = gather(term, nrow, nchip, 5).reshape(NSUP, W, W)
    return mine, diag_inv - diag


def solution(mesh):
    placed = (P("prow", "pcol"), P(None, "prow", None), P(), P())
    return jax.shard_map(
        functools.partial(per_device, mesh.shape["prow"], mesh.shape["pcol"]),
        mesh=mesh,
        in_specs=placed,
        out_specs=(P(None, ("prow", "pcol"), None), P()),
        check_vma=False,
    )
```
